512 devices in a mesh: context: 64 (over x, z), tensor: 8 (over y, core).
Axes of the slice: x: 4, y: 4, z: 16, core: 2. Of those that a mesh axis runs over, the one named last changes fastest.
Arguments:
- sequence: bfloat16 [256, 32768], P('tensor', 'context'), may hold values from -6 to 6
- proj_in: bfloat16 [3, 256, 256], P(None, None, 'tensor'), may hold values from -0.375 to 0.375
- conv_filter: float32 [256, 32768], P('tensor', 'context'), may hold values from -2 to 2
- skip_gain: float32 [256], P('tensor'), may hold values from -1 to 1
- proj_out: bfloat16 [256, 256], P('tensor'), may hold values from -0.375 to 0.375
Outputs:
- mixed_out: bfloat16 [256, 32768], P(None, 'context')
The draws below stay inside these ranges and needn't reach their ends.
All inputs are finite; a program needn't handle non-finite values.
Results may differ from the reference program's by a relative error of at most 0.0049.
Values may be sent and summed in bfloat16 or wider, within the bound.
No kernel may reach another device: no remote copies, remote signals or barrier semaphores. Data moves between devices by JAX's collectives and lax.ppermute only.
A program may use at most 64 MiB of HBM per device.

```python
import math
import jax
import jax.numpy as jnp

MODEL_WIDTH = 256
SEQUENCE_LENGTH = 32768


def draw_conv_filter(key, part):
    key = jax.random.fold_in(key, 7)
    random_subkeys = jax.random.split(key, 3)
    random_part = jax.random.truncated_normal(random_subkeys[0], -4.0, 4.0, (MODEL_WIDTH, SEQUENCE_LENGTH), jnp.float32)
    slow_rate = 0.5
    fast_rate = 6.0
    decay_rates = jnp.exp(jax.random.uniform(random_subkeys[1], (MODEL_WIDTH, 1), jnp.float32, math.log(slow_rate), math.log(fast_rate)))
    positions = jnp.arange(SEQUENCE_LENGTH, dtype=jnp.float32)[None, :]
    filter_envelope = jnp.exp(-decay_rates * positions / SEQUENCE_LENGTH)
    energy = jnp.expm1(-2.0 * decay_rates) / jnp.expm1(-2.0 * decay_rates / SEQUENCE_LENGTH)
    filter_envelope = filter_envelope / jnp.sqrt(energy)
    spike_positions = jax.random.randint(random_subkeys[2], (MODEL_WIDTH, 4), 0, SEQUENCE_LENGTH)
    integer_steps = jnp.arange(SEQUENCE_LENGTH, dtype=jnp.int32)[None, :]
    for spike_index in range(4):
        filter_envelope = filter_envelope * jnp.where(integer_steps >= spike_positions[:, spike_index:spike_index + 1], 0.6, 1.0)
    return random_part * filter_envelope


def block_scale(key, dims, cuts, low, high):
    gain = 1.0
    for axis_at, parts in cuts:
        steps = jax.random.uniform(jax.random.fold_in(jax.random.fold_in(key, 6), axis_at), (parts,), jnp.float32, low / len(cuts), high / len(cuts))
        gain = gain * jnp.repeat(jnp.exp(steps), dims[axis_at] // parts).reshape((-1,) + (1,) * (len(dims) - 1 - axis_at))
    return gain


def gaussian(key, shape, spread, reach, shards=(), held_as=jnp.bfloat16):
    values = jax.random.normal(key, shape, jnp.float32) * spread
    if len(shards) > 0:
        values = block_scale(key, shape, shards, -0.22, 0.18) * values
    return jnp.clip(values, min=-reach, max=reach).astype(held_as)


def setup_inputs(seed: int = 0) -> dict:
    splits = jax.random.split(jax.random.key(seed), 6)
    sequence = gaussian(splits[0], (MODEL_WIDTH, SEQUENCE_LENGTH), 1.0, 6.0, ((0, 8), (1, 64)))
    proj_in = gaussian(splits[1], (3, MODEL_WIDTH, MODEL_WIDTH), MODEL_WIDTH ** -0.5, 0.375, ((2, 8),))
    conv_filter = draw_conv_filter(jax.random.fold_in(splits[5], 71), 0)
    skip_gain = jnp.clip(jax.random.uniform(splits[3], (MODEL_WIDTH,), jnp.float32, -1.0, 1.0) * block_scale(splits[3], (MODEL_WIDTH,), ((0, 8),), -0.4, 0.0), -1.0, 1.0)
    proj_out = gaussian(splits[4], (MODEL_WIDTH, MODEL_WIDTH), MODEL_WIDTH ** -0.5, 0.375, ((0, 8),))
    return {"sequence": sequence, "proj_in": proj_in, "conv_filter": conv_filter, "skip_gain": skip_gain, "proj_out": proj_out}


def reference(sequence, proj_in, conv_filter, skip_gain, proj_out):
    projected = jnp.einsum("bio,il->bol", proj_in.astype(jnp.float32), sequence.astype(jnp.float32))
    gated_value = projected[2] * projected[0]
    spectrum = jnp.fft.rfft(gated_value, n=2 * SEQUENCE_LENGTH, axis=-1) * jnp.fft.rfft(conv_filter, n=2 * SEQUENCE_LENGTH, axis=-1)
    convolved = jnp.fft.irfft(spectrum, n=2 * SEQUENCE_LENGTH, axis=-1)[:, :SEQUENCE_LENGTH]
    convolved = convolved + skip_gain[:, None] * gated_value
    out_gated = (convolved * projected[1]).astype(jnp.bfloat16)
    mixed_out = jnp.dot(proj_out.T, out_gated, preferred_element_type=jnp.float32)
    return mixed_out.astype(jnp.bfloat16)
```

```python
import math

import jax
import jax.numpy as jnp
import numpy as np
from jax import lax
from jax.experimental import pallas as pl
from jax.experimental.pallas import tpu as pltpu
from jax.sharding import PartitionSpec as P

ROWS = 256
LANES = 128
LENGTH = ROWS * LANES
PIECE = 4
RANKS = ROWS // PIECE


def split_table(table):
    upper = table.astype(jnp.bfloat16)
    lower = (table - upper.astype(np.float64)).astype(jnp.bfloat16)
    return upper, lower


def tables():
    slot = np.arange(ROWS)
    row = (slot % RANKS) * PIECE + slot // RANKS
    low = np.arange(ROWS)
    lane = np.arange(LANES)
    turn = 2.0 * np.pi * np.outer(low + 0.25, row) / ROWS
    outer = np.concatenate([np.cos(turn), -np.sin(turn)], axis=0)
    turn = 2.0 * np.pi * np.outer(low + 0.25, lane) / LENGTH
    twist = np.stack([np.cos(turn), np.sin(turn)]).astype(np.float32)
    turn = 2.0 * np.pi * (np.outer(lane, lane) % LANES) / LANES
    cos_part, sin_part = np.cos(turn), np.sin(turn)
    inner = np.block([[cos_part, -sin_part], [sin_part, cos_part]])
    return (
        *split_table(outer),
        *split_table(outer.T / LENGTH),
        *split_table(inner),
        *split_table(inner.T),
        twist,
    )


def dot(left, right):
    return jnp.dot(left, right, preferred_element_type=jnp.float32)


def split_value(value):
    upper = value.astype(jnp.bfloat16)
    lower = (value - upper.astype(jnp.float32)).astype(jnp.bfloat16)
    return upper, lower


def project_kernel(gathered_ref, proj_ref, filter_ref, send_ref, gated_ref, gate_ref, rows_ref):
    width = gathered_ref.shape[0]
    tok_len = filter_ref.shape[1]
    channels = filter_ref.shape[0]
    sequence = gathered_ref[:, :tok_len]
    first, gate, value = [
        lax.dot_general(
            proj_ref[index], sequence, (((0,), (0,)), ((), ())), preferred_element_type=jnp.float32
        )
        for index in range(3)
    ]
    gated = value * first
    gated_ref[...] = gated
    gate_ref[...] = gate
    for piece in range(PIECE):
        cut = slice(piece * LANES, (piece + 1) * LANES)
        for half in range(2):
            span = slice(half * channels, (half + 1) * channels)
            rows_ref[span, piece, :] = gated[:, cut]
            rows_ref[span, PIECE + piece, :] = filter_ref[:, cut]
    send_ref[...] = rows_ref[...].astype(jnp.bfloat16)


def convolve_kernel(
    half_ref, recv_ref, fwd_hi, fwd_lo, back_hi, back_lo, in_hi, in_lo, out_hi, out_lo, twist_ref,
    send_ref, rows_ref, result_ref,
):
    rows_ref[...] = recv_ref[...].astype(jnp.float32)
    both = jnp.concatenate(
        [
            jnp.concatenate([rows_ref[:, piece, :], rows_ref[:, PIECE + piece, :]], axis=1)
            for piece in range(PIECE)
        ],
        axis=0,
    ).astype(jnp.bfloat16)
    cos_part = twist_ref[0]
    sin_part = twist_ref[1]
    outer = dot(fwd_hi[...], both) + dot(fwd_lo[...], both)
    real, imag = outer[:ROWS], outer[ROWS:]
    turned = []
    for cut in (slice(0, LANES), slice(LANES, 2 * LANES)):
        turned.append(
            jnp.concatenate(
                [
                    real[:, cut] * cos_part + imag[:, cut] * sin_part,
                    imag[:, cut] * cos_part - real[:, cut] * sin_part,
                ],
                axis=1,
            )
        )
    upper, lower = split_value(jnp.concatenate(turned, axis=0))
    spectra = dot(upper, in_hi[...]) + dot(lower, in_hi[...]) + dot(upper, in_lo[...])
    source_real, source_imag = spectra[:ROWS, :LANES], spectra[:ROWS, LANES:]
    filter_real, filter_imag = spectra[ROWS:, :LANES], spectra[ROWS:, LANES:]
    product = jnp.concatenate(
        [
            source_real * filter_real - source_imag * filter_imag,
            source_real * filter_imag + source_imag * filter_real,
        ],
        axis=1,
    )
    upper, lower = split_value(product)
    inner = dot(upper, out_hi[...]) + dot(lower, out_hi[...]) + dot(upper, out_lo[...])
    real, imag = inner[:, :LANES], inner[:, LANES:]
    upper, lower = split_value(
        jnp.concatenate(
            [real * cos_part - imag * sin_part, imag * cos_part + real * sin_part], axis=0
        )
    )
    span = pl.ds(pl.multiple_of(half_ref[0] * (ROWS // 2), ROWS // 2), ROWS // 2)
    left_hi, left_lo = back_hi[span, :], back_lo[span, :]
    result = dot(left_hi, upper) + dot(left_hi, lower) + dot(left_lo, upper)
    for piece in range(PIECE // 2):
        result_ref[:, piece, :] = result[piece * RANKS : (piece + 1) * RANKS]
    send_ref[...] = result_ref[...].astype(jnp.bfloat16)


def gate_kernel(recv_ref, gated_ref, gate_ref, skip_ref, send_ref, rows_ref):
    channels = gated_ref.shape[0]
    rows_ref[...] = recv_ref[...].astype(jnp.float32)
    convolved = jnp.concatenate(
        [
            rows_ref[half * channels : (half + 1) * channels, piece, :]
            for half in range(2)
            for piece in range(PIECE // 2)
        ],
        axis=1,
    )
    convolved = convolved + skip_ref[...] * gated_ref[...]
    out_gated = (convolved * gate_ref[...]).astype(jnp.bfloat16)
    for copy in range(send_ref.shape[0]):
        send_ref[copy] = out_gated


def whole(count):
    return [pl.BlockSpec(memory_space=pltpu.VMEM) for _ in range(count)]


def shards(sequence, proj_in, conv_filter, skip_gain, proj_out):
    channels, tok_len = sequence.shape
    width = proj_out.shape[1]
    groups = lax.axis_size("tensor")
    ranks = lax.axis_size("context")
    rank = lax.axis_index("context")
    half = (rank // (ranks // 2)).astype(jnp.int32).reshape(1)

    packed = jnp.concatenate([sequence, proj_out], axis=1)
    gathered = lax.all_to_all(
        jnp.broadcast_to(packed[None], (groups, *packed.shape)), "tensor", 0, 0, tiled=True
    ).reshape(width, tok_len + width)

    send, gated, gate = pl.pallas_call(
        project_kernel,
        out_shape=(
            jax.ShapeDtypeStruct((ranks, 2 * PIECE, LANES), jnp.bfloat16),
            jax.ShapeDtypeStruct((channels, tok_len), jnp.float32),
            jax.ShapeDtypeStruct((channels, tok_len), jnp.float32),
        ),
        in_specs=whole(3),
        out_specs=tuple(whole(3)),
        scratch_shapes=[pltpu.VMEM((ranks, 2 * PIECE, LANES), jnp.float32)],
        compiler_params=pltpu.CompilerParams(vmem_limit_bytes=16 * 2**20),
        name="project",
    )(gathered, proj_in, conv_filter)

    recv = lax.all_to_all(send, "context", 0, 0, tiled=True)

    constants = [jnp.asarray(table) for table in tables()]
    send = pl.pallas_call(
        convolve_kernel,
        out_shape=jax.ShapeDtypeStruct((ranks, PIECE // 2, LANES), jnp.bfloat16),
        in_specs=[pl.BlockSpec(memory_space=pltpu.SMEM)] + whole(1 + len(constants)),
        out_specs=whole(1)[0],
        scratch_shapes=[
            pltpu.VMEM((ranks, 2 * PIECE, LANES), jnp.float32),
            pltpu.VMEM((ranks, PIECE // 2, LANES), jnp.float32),
        ],
        compiler_params=pltpu.CompilerParams(vmem_limit_bytes=24 * 2**20),
        name="convolve",
    )(half, recv, *constants)

    recv = lax.all_to_all(send, "context", 0, 0, tiled=True)

    send = pl.pallas_call(
        gate_kernel,
        out_shape=jax.ShapeDtypeStruct((groups, channels, tok_len), jnp.bfloat16),
        in_specs=whole(4),
        out_specs=whole(1)[0],
        scratch_shapes=[pltpu.VMEM((ranks, PIECE // 2, LANES), jnp.float32)],
        compiler_params=pltpu.CompilerParams(vmem_limit_bytes=16 * 2**20),
        name="gate",
    )(recv, gated, gate, skip_gain.reshape(channels, 1))

    out_gated = lax.all_to_all(send, "tensor", 0, 0, tiled=True).reshape(width, tok_len)
    mixed = lax.dot_general(
        gathered[:, tok_len:],
        out_gated,
        (((0,), (0,)), ((), ())),
        preferred_element_type=jnp.float32,
    )
    return mixed.astype(jnp.bfloat16)


def solution(mesh):
    return jax.shard_map(
        shards,
        mesh=mesh,
        in_specs=(
            P("tensor", "context"),
            P(None, None, "tensor"),
            P("tensor", "context"),
            P("tensor"),
            P("tensor", None),
        ),
        out_specs=P(None, "context"),
        check_vma=False,
    )
```

```python
import math

import jax
import jax.numpy as jnp
import numpy as np
from jax import lax
from jax.experimental import pallas as pl
from jax.experimental.pallas import tpu as pltpu
from jax.sharding import PartitionSpec as P

ROWS = 256
LANES = 128
LENGTH = ROWS * LANES
PIECE = 4
RANKS = ROWS // PIECE
LINES, RING = 4, 16
CHANNELS = RANKS // 2

TURN = 2
HALVES = [
    [(outer + TURN) % LINES * RING + inner for outer in range(LINES) for inner in ring]
    for ring in (range(RING // 2, RING), range(RING // 2 - 1, -1, -1))
]
ORDER = HALVES[0] + HALVES[1]


def split_table(table):
    upper = table.astype(jnp.bfloat16)
    lower = (table - upper.astype(np.float64)).astype(jnp.bfloat16)
    return upper, lower


def tables():
    come = np.concatenate([np.asarray(ORDER) * PIECE + piece for piece in range(PIECE)])
    go = np.concatenate(
        [np.asarray(half) * PIECE + piece for half in HALVES for piece in range(PIECE)]
    )
    low = np.arange(ROWS)
    lane = np.arange(LANES)

    def outer(row):
        turn = 2.0 * np.pi * np.outer(low + 0.25, row) / ROWS
        return np.concatenate([np.cos(turn), -np.sin(turn)], axis=0)

    turn = 2.0 * np.pi * np.outer(low + 0.25, lane) / LENGTH
    twist = np.stack([np.cos(turn), np.sin(turn)]).astype(np.float32)
    turn = 2.0 * np.pi * (np.outer(lane, lane) % LANES) / LANES
    cos_part, sin_part = np.cos(turn), np.sin(turn)
    inner = np.block([[cos_part, -sin_part], [sin_part, cos_part]])
    return (
        *split_table(outer(come)),
        *split_table(outer(go).T / LENGTH),
        *split_table(inner),
        *split_table(inner.T),
        twist,
    )


def dot(left, right):
    return jnp.dot(left, right, preferred_element_type=jnp.float32)


def split_value(value):
    upper = value.astype(jnp.bfloat16)
    lower = (value - upper.astype(jnp.float32)).astype(jnp.bfloat16)
    return upper, lower


def spread_kernel(sequence_ref, proj_ref, send_ref):
    tok_len = sequence_ref.shape[1]
    for copy in range(send_ref.shape[0]):
        send_ref[copy, :, :tok_len] = sequence_ref[...]
        send_ref[copy, :, tok_len:] = proj_ref[...]


def project_kernel(
    gathered_ref, proj_ref, filter_ref, skip_ref, send_ref, gate_ref, direct_ref, rows_ref
):
    channels, tok_len = filter_ref.shape
    sequence = gathered_ref[:, :tok_len]
    first, gate, value = [
        lax.dot_general(
            proj_ref[index], sequence, (((0,), (0,)), ((), ())), preferred_element_type=jnp.float32
        )
        for index in range(3)
    ]
    gated = value * first
    gate_ref[...] = gate
    direct_ref[...] = skip_ref[...] * gated
    for piece in range(PIECE):
        cut = slice(piece * LANES, (piece + 1) * LANES)
        for half in range(2):
            span = slice(half * channels, (half + 1) * channels)
            rows_ref[span, piece, :] = gated[:, cut]
            rows_ref[span, PIECE + piece, :] = filter_ref[:, cut]
    send_ref[...] = rows_ref[...].astype(jnp.bfloat16)


def convolve_kernel(
    half_ref, recv_ref, fwd_hi, fwd_lo, back_hi, back_lo, in_hi, in_lo, out_hi, out_lo, twist_ref,
    send_ref, rows_ref, result_ref,
):
    rows_ref[...] = recv_ref[...].astype(jnp.float32)
    both = jnp.concatenate(
        [
            jnp.concatenate([rows_ref[:, piece, :], rows_ref[:, PIECE + piece, :]], axis=1)
            for piece in range(PIECE)
        ],
        axis=0,
    ).astype(jnp.bfloat16)
    cos_part = twist_ref[0]
    sin_part = twist_ref[1]
    outer = dot(fwd_hi[...], both) + dot(fwd_lo[...], both)
    real, imag = outer[:ROWS], outer[ROWS:]
    turned = []
    for cut in (slice(0, LANES), slice(LANES, 2 * LANES)):
        turned.append(
            jnp.concatenate(
                [
                    real[:, cut] * cos_part + imag[:, cut] * sin_part,
                    imag[:, cut] * cos_part - real[:, cut] * sin_part,
                ],
                axis=1,
            )
        )
    upper, lower = split_value(jnp.concatenate(turned, axis=0))
    spectra = dot(upper, in_hi[...]) + dot(lower, in_hi[...]) + dot(upper, in_lo[...])
    source_real, source_imag = spectra[:ROWS, :LANES], spectra[:ROWS, LANES:]
    filter_real, filter_imag = spectra[ROWS:, :LANES], spectra[ROWS:, LANES:]
    product = jnp.concatenate(
        [
            source_real * filter_real - source_imag * filter_imag,
            source_real * filter_imag + source_imag * filter_real,
        ],
        axis=1,
    )
    upper, lower = split_value(product)
    inner = dot(upper, out_hi[...]) + dot(lower, out_hi[...]) + dot(upper, out_lo[...])
    real, imag = inner[:, :LANES], inner[:, LANES:]
    upper, lower = split_value(
        jnp.concatenate(
            [real * cos_part - imag * sin_part, imag * cos_part + real * sin_part], axis=0
        )
    )
    span = pl.ds(pl.multiple_of(half_ref[0] * (ROWS // 2), ROWS // 2), ROWS // 2)
    left_hi, left_lo = back_hi[span, :], back_lo[span, :]
    result = dot(left_hi, upper) + dot(left_hi, lower) + dot(left_lo, upper)
    for piece in range(PIECE):
        result_ref[:, piece, :] = result[piece * CHANNELS : (piece + 1) * CHANNELS]
    send_ref[...] = result_ref[...].astype(jnp.bfloat16)


def gate_kernel(recv_ref, gate_ref, direct_ref, send_ref, rows_ref):
    rows_ref[...] = recv_ref[...].astype(jnp.float32)
    convolved = jnp.concatenate([rows_ref[:, piece, :] for piece in range(PIECE)], axis=1)
    out_gated = ((convolved + direct_ref[...]) * gate_ref[...]).astype(jnp.bfloat16)
    for copy in range(send_ref.shape[0]):
        send_ref[copy] = out_gated


def whole(count):
    return [pl.BlockSpec(memory_space=pltpu.VMEM) for _ in range(count)]


def shards(sequence, proj_in, conv_filter, skip_gain, proj_out):
    channels, tok_len = sequence.shape
    width = proj_out.shape[1]
    groups = lax.axis_size("tensor")
    ranks = lax.axis_size("context")
    half = (1 - lax.axis_index("context") % RING // (RING // 2)).astype(jnp.int32).reshape(1)

    send = pl.pallas_call(
        spread_kernel,
        out_shape=pltpu.VMEM((groups, channels, tok_len + width), jnp.bfloat16),
        in_specs=whole(2),
        out_specs=whole(1)[0],
        name="spread",
    )(sequence, proj_out)

    gathered = lax.all_to_all(send, "tensor", 0, 0, tiled=True).reshape(width, tok_len + width)

    send, gate, direct = pl.pallas_call(
        project_kernel,
        out_shape=(
            pltpu.VMEM((ranks, 2 * PIECE, LANES), jnp.bfloat16),
            pltpu.VMEM((channels, tok_len), jnp.float32),
            pltpu.VMEM((channels, tok_len), jnp.float32),
        ),
        in_specs=whole(4),
        out_specs=tuple(whole(3)),
        scratch_shapes=[pltpu.VMEM((ranks, 2 * PIECE, LANES), jnp.float32)],
        compiler_params=pltpu.CompilerParams(vmem_limit_bytes=16 * 2**20),
        name="project",
    )(gathered, proj_in, conv_filter, skip_gain.reshape(channels, 1))

    recv = lax.all_to_all(send, "context", 0, 0, axis_index_groups=[ORDER], tiled=True)

    constants = [jnp.asarray(table) for table in tables()]
    send = pl.pallas_call(
        convolve_kernel,
        out_shape=pltpu.VMEM((channels, PIECE, LANES), jnp.bfloat16),
        in_specs=[pl.BlockSpec(memory_space=pltpu.SMEM)] + whole(1 + len(constants)),
        out_specs=whole(1)[0],
        scratch_shapes=[
            pltpu.VMEM((ranks, 2 * PIECE, LANES), jnp.float32),
            pltpu.VMEM((channels, PIECE, LANES), jnp.float32),
        ],
        compiler_params=pltpu.CompilerParams(vmem_limit_bytes=24 * 2**20),
        name="convolve",
    )(half, recv, *constants)

    recv = lax.all_to_all(send, "context", 0, 0, axis_index_groups=HALVES, tiled=True)

    send = pl.pallas_call(
        gate_kernel,
        out_shape=pltpu.VMEM((groups, channels, tok_len), jnp.bfloat16),
        in_specs=whole(3),
        out_specs=whole(1)[0],
        scratch_shapes=[pltpu.VMEM((channels, PIECE, LANES), jnp.float32)],
        compiler_params=pltpu.CompilerParams(vmem_limit_bytes=16 * 2**20),
        name="gate",
    )(recv, gate, direct)

    out_gated = lax.all_to_all(send, "tensor", 0, 0, tiled=True).reshape(width, tok_len)
    mixed = lax.dot_general(
        gathered[:, tok_len:],
        out_gated,
        (((0,), (0,)), ((), ())),
        preferred_element_type=jnp.float32,
    )
    return mixed.astype(jnp.bfloat16)


def solution(mesh):
    return jax.shard_map(
        shards,
        mesh=mesh,
        in_specs=(
            P("tensor", "context"),
            P(None, None, "tensor"),
            P("tensor", "context"),
            P("tensor"),
            P("tensor", None),
        ),
        out_specs=P(None, "context"),
        check_vma=False,
    )
```

```python
import math

import jax
import jax.numpy as jnp
import numpy as np
from jax import lax
from jax.experimental import pallas as pl
from jax.experimental.pallas import tpu as pltpu
from jax.sharding import PartitionSpec as P

ROWS = 256
LANES = 128
LENGTH = ROWS * LANES
PIECE = 4
RANKS = ROWS // PIECE
LINES, RING = 4, 16
CHANNELS = RANKS // 2

TURN = 2
HALVES = [
    [(outer + TURN) % LINES * RING + inner for outer in range(LINES) for inner in ring]
    for ring in ((10, 11, 12, 13, 14, 15, 8, 9), (7, 6, 5, 4, 3, 2, 1, 0))
]
ORDER = HALVES[0] + HALVES[1]

GROUP = [4, 5, 6, 7, 0, 1, 2, 3]


def split_table(table):
    upper = table.astype(jnp.bfloat16)
    lower = (table - upper.astype(np.float64)).astype(jnp.bfloat16)
    return upper, lower


def tables():
    come = np.concatenate([np.asarray(ORDER) * PIECE + piece for piece in range(PIECE)])
    go = np.concatenate(
        [np.asarray(half) * PIECE + piece for half in HALVES for piece in range(PIECE)]
    )
    low = np.arange(ROWS)
    lane = np.arange(LANES)

    def outer(row):
        turn = 2.0 * np.pi * np.outer(low + 0.25, row) / ROWS
        return np.concatenate([np.cos(turn), -np.sin(turn)], axis=0)

    turn = 2.0 * np.pi * np.outer(low + 0.25, lane) / LENGTH
    twist = np.stack([np.cos(turn), np.sin(turn)]).astype(np.float32)
    turn = 2.0 * np.pi * (np.outer(lane, lane) % LANES) / LANES
    cos_part, sin_part = np.cos(turn), np.sin(turn)
    inner = np.block([[cos_part, -sin_part], [sin_part, cos_part]])
    return (
        *split_table(outer(come)),
        *split_table(outer(go).T / LENGTH),
        *split_table(inner),
        *split_table(inner.T),
        twist,
    )


def dot(left, right):
    return jnp.dot(left, right, preferred_element_type=jnp.float32)


def split_value(value):
    upper = value.astype(jnp.bfloat16)
    lower = (value - upper.astype(jnp.float32)).astype(jnp.bfloat16)
    return upper, lower


def spread_kernel(sequence_ref, proj_ref, send_ref):
    tok_len = sequence_ref.shape[1]
    for copy in range(send_ref.shape[0]):
        send_ref[copy, :, :tok_len] = sequence_ref[...]
        send_ref[copy, :, tok_len:] = proj_ref[...]


def project_kernel(
    gathered_ref, proj_ref, filter_ref, skip_ref, send_ref, gate_ref, direct_ref, rows_ref
):
    channels, tok_len = filter_ref.shape
    sequence = jnp.concatenate(
        [
            gathered_ref[place * channels : (place + 1) * channels, :tok_len]
            for place in np.argsort(GROUP).tolist()
        ],
        axis=0,
    )
    first, gate, value = [dot(proj_ref[index], sequence) for index in range(3)]
    gated = value * first
    gate_ref[...] = gate
    place = lax.broadcasted_iota(jnp.int32, (channels, channels), 0)
    other = lax.broadcasted_iota(jnp.int32, (channels, channels), 1)
    skip = jnp.sum(jnp.where(place == other, skip_ref[...], 0.0), axis=1, keepdims=True)
    direct_ref[...] = skip * gated
    for piece in range(PIECE):
        cut = slice(piece * LANES, (piece + 1) * LANES)
        for half in range(2):
            span = slice(half * channels, (half + 1) * channels)
            rows_ref[span, piece, :] = gated[:, cut]
            rows_ref[span, PIECE + piece, :] = filter_ref[:, cut]
    send_ref[...] = rows_ref[...].astype(jnp.bfloat16)


def convolve_kernel(
    recv_ref, fwd_hi, fwd_lo, back_hi, back_lo, in_hi, in_lo, out_hi, out_lo, twist_ref,
    send_ref, rows_ref, result_ref,
):
    rows_ref[...] = recv_ref[...].astype(jnp.float32)
    both = jnp.concatenate(
        [
            jnp.concatenate([rows_ref[:, piece, :], rows_ref[:, PIECE + piece, :]], axis=1)
            for piece in range(PIECE)
        ],
        axis=0,
    ).astype(jnp.bfloat16)
    cos_part = twist_ref[0]
    sin_part = twist_ref[1]
    outer = dot(fwd_hi[...], both) + dot(fwd_lo[...], both)
    real, imag = outer[:ROWS], outer[ROWS:]
    turned = []
    for cut in (slice(0, LANES), slice(LANES, 2 * LANES)):
        turned.append(
            jnp.concatenate(
                [
                    real[:, cut] * cos_part + imag[:, cut] * sin_part,
                    imag[:, cut] * cos_part - real[:, cut] * sin_part,
                ],
                axis=1,
            )
        )
    upper, lower = split_value(jnp.concatenate(turned, axis=0))
    spectra = dot(upper, in_hi[...]) + dot(lower, in_hi[...]) + dot(upper, in_lo[...])
    source_real, source_imag = spectra[:ROWS, :LANES], spectra[:ROWS, LANES:]
    filter_real, filter_imag = spectra[ROWS:, :LANES], spectra[ROWS:, LANES:]
    product = jnp.concatenate(
        [
            source_real * filter_real - source_imag * filter_imag,
            source_real * filter_imag + source_imag * filter_real,
        ],
        axis=1,
    )
    upper, lower = split_value(product)
    inner = dot(upper, out_hi[...]) + dot(lower, out_hi[...]) + dot(upper, out_lo[...])
    real, imag = inner[:, :LANES], inner[:, LANES:]
    upper, lower = split_value(
        jnp.concatenate(
            [real * cos_part - imag * sin_part, imag * cos_part + real * sin_part], axis=0
        )
    )
    half = 1 - lax.axis_index("context") % RING // (RING // 2)
    span = pl.ds(pl.multiple_of(half * (ROWS // 2), ROWS // 2), ROWS // 2)
    both = dot(back_hi[span, :], jnp.concatenate([upper, lower], axis=1))
    result = both[:, :LANES] + both[:, LANES:] + dot(back_lo[span, :], upper)
    for piece in range(PIECE):
        result_ref[:, piece, :] = result[piece * CHANNELS : (piece + 1) * CHANNELS]
    send_ref[...] = result_ref[...].astype(jnp.bfloat16)


def gate_kernel(recv_ref, gate_ref, direct_ref, send_ref, rows_ref):
    rows_ref[...] = recv_ref[...].astype(jnp.float32)
    convolved = jnp.concatenate([rows_ref[:, piece, :] for piece in range(PIECE)], axis=1)
    out_gated = ((convolved + direct_ref[...]) * gate_ref[...]).astype(jnp.bfloat16)
    for copy in range(send_ref.shape[0]):
        send_ref[copy] = out_gated


def whole(count):
    return [pl.BlockSpec(memory_space=pltpu.VMEM) for _ in range(count)]


def shards(sequence, proj_in, conv_filter, skip_gain, proj_out):
    channels, tok_len = sequence.shape
    width = proj_out.shape[1]
    groups = lax.axis_size("tensor")
    ranks = lax.axis_size("context")

    send = pl.pallas_call(
        spread_kernel,
        out_shape=pltpu.VMEM((groups, channels, tok_len + width), jnp.bfloat16),
        in_specs=whole(2),
        out_specs=whole(1)[0],
        name="spread",
    )(sequence, proj_out)

    gathered = lax.all_to_all(send, "tensor", 0, 0, axis_index_groups=[GROUP], tiled=True)
    gathered = gathered.reshape(width, tok_len + width)

    send, gate, direct = pl.pallas_call(
        project_kernel,
        out_shape=(
            pltpu.VMEM((ranks, 2 * PIECE, LANES), jnp.bfloat16),
            pltpu.VMEM((channels, tok_len), jnp.float32),
            pltpu.VMEM((channels, tok_len), jnp.float32),
        ),
        in_specs=whole(4),
        out_specs=tuple(whole(3)),
        scratch_shapes=[pltpu.VMEM((ranks, 2 * PIECE, LANES), jnp.float32)],
        compiler_params=pltpu.CompilerParams(vmem_limit_bytes=16 * 2**20),
        name="project",
    )(gathered, jnp.swapaxes(proj_in, 1, 2), conv_filter, skip_gain.reshape(1, channels))

    recv = lax.all_to_all(send, "context", 0, 0, axis_index_groups=[ORDER], tiled=True)

    constants = [jnp.asarray(table) for table in tables()]
    send = pl.pallas_call(
        convolve_kernel,
        out_shape=pltpu.VMEM((channels, PIECE, LANES), jnp.bfloat16),
        in_specs=whole(1 + len(constants)),
        out_specs=whole(1)[0],
        scratch_shapes=[
            pltpu.VMEM((ranks, 2 * PIECE, LANES), jnp.float32),
            pltpu.VMEM((channels, PIECE, LANES), jnp.float32),
        ],
        compiler_params=pltpu.CompilerParams(vmem_limit_bytes=24 * 2**20),
        name="convolve",
    )(recv, *constants)

    recv = lax.all_to_all(send, "context", 0, 0, axis_index_groups=HALVES, tiled=True)

    send = pl.pallas_call(
        gate_kernel,
        out_shape=pltpu.VMEM((groups, channels, tok_len), jnp.bfloat16),
        in_specs=whole(3),
        out_specs=whole(1)[0],
        scratch_shapes=[pltpu.VMEM((channels, PIECE, LANES), jnp.float32)],
        compiler_params=pltpu.CompilerParams(vmem_limit_bytes=16 * 2**20),
        name="gate",
    )(recv, gate, direct)

    out_gated = lax.all_to_all(send, "tensor", 0, 0, axis_index_groups=[GROUP], tiled=True)
    mixed = lax.dot_general(
        gathered[:, tok_len:],
        out_gated.reshape(width, tok_len),
        (((0,), (0,)), ((), ())),
        preferred_element_type=jnp.float32,
    )
    return mixed.astype(jnp.bfloat16)


def solution(mesh):
    return jax.shard_map(
        shards,
        mesh=mesh,
        in_specs=(
            P("tensor", "context"),
            P(None, None, "tensor"),
            P("tensor", "context"),
            P("tensor"),
            P("tensor", None),
        ),
        out_specs=P(None, "context"),
        check_vma=False,
    )
```

```python
import math

import jax
import jax.numpy as jnp
import numpy as np
from jax import lax
from jax.experimental import pallas as pl
from jax.experimental.pallas import tpu as pltpu
from jax.sharding import PartitionSpec as P

ROWS = 256
LANES = 128
LENGTH = ROWS * LANES
PIECE = 4
RANKS = ROWS // PIECE
LINES, RING = 4, 16
CHANNELS = RANKS // 2

TURN = 2
HALVES = [
    [(outer + TURN) % LINES * RING + inner for outer in range(LINES) for inner in ring]
    for ring in ((10, 11, 12, 13, 14, 15, 8, 9), (6, 7, 5, 4, 3, 2, 1, 0))
]
ORDER = HALVES[0] + HALVES[1]

GROUP = [4, 5, 6, 7, 0, 1, 2, 3]


def split_table(table):
    upper = table.astype(jnp.bfloat16)
    lower = (table - upper.astype(np.float64)).astype(jnp.bfloat16)
    return upper, lower


def tables():
    come = np.concatenate([np.asarray(ORDER) * PIECE + piece for piece in range(PIECE)])
    go = np.concatenate(
        [np.asarray(half) * PIECE + piece for half in HALVES for piece in range(PIECE)]
    )
    low = np.arange(ROWS)
    lane = np.arange(LANES)

    def outer(row):
        turn = 2.0 * np.pi * np.outer(low + 0.25, row) / ROWS
        return np.concatenate([np.cos(turn), -np.sin(turn)], axis=0)

    turn = 2.0 * np.pi * np.outer(low + 0.25, lane) / LENGTH
    twist = np.stack([np.cos(turn), np.sin(turn)]).astype(np.float32)
    turn = 2.0 * np.pi * (np.outer(lane, lane) % LANES) / LANES
    cos_part, sin_part = np.cos(turn), np.sin(turn)
    inner = np.block([[cos_part, -sin_part], [sin_part, cos_part]])
    return (
        *split_table(outer(come)),
        *split_table(outer(go).T / LENGTH),
        *split_table(inner),
        *split_table(inner.T),
        twist,
    )


def dot(left, right):
    return jnp.dot(left, right, preferred_element_type=jnp.float32)


def split_value(value):
    upper = value.astype(jnp.bfloat16)
    lower = (value - upper.astype(jnp.float32)).astype(jnp.bfloat16)
    return upper, lower


def halves(part, rows):
    middle = rows // 2
    return jnp.concatenate([part(slice(0, middle)), part(slice(middle, rows))], axis=0)


def inner_transform(value, table_hi, table_lo):
    upper, lower = split_value(value)
    return halves(
        lambda cut: dot(upper[cut], table_hi[...])
        + dot(lower[cut], table_hi[...])
        + dot(upper[cut], table_lo[...]),
        value.shape[0],
    )


def spread_kernel(
    sequence_ref, proj_ref, filter_ref, skip_ref, out_ref,
    send_ref, proj_copy, filter_copy, skip_copy, out_copy,
):
    tok_len = sequence_ref.shape[1]
    for copy in range(send_ref.shape[0]):
        send_ref[copy, :, :tok_len] = sequence_ref[...]
        if send_ref.shape[2] > tok_len:
            send_ref[copy, :, tok_len:] = out_ref[...]
    proj_copy[...] = proj_ref[...]
    filter_copy[...] = filter_ref[...]
    skip_copy[...] = skip_ref[...]
    out_copy[...] = out_ref[...]


def project_kernel(
    gathered_ref, proj_ref, filter_ref, skip_ref, own_ref,
    send_ref, gate_ref, direct_ref, out_ref, rows_ref,
):
    channels, tok_len = filter_ref.shape
    sequence = jnp.concatenate(
        [
            gathered_ref[place * channels : (place + 1) * channels, :tok_len]
            for place in np.argsort(GROUP).tolist()
        ],
        axis=0,
    )
    first, gate, value = [dot(proj_ref[index], sequence) for index in range(3)]
    gated = value * first
    gate_ref[...] = gate
    place = lax.broadcasted_iota(jnp.int32, (channels, channels), 0)
    other = lax.broadcasted_iota(jnp.int32, (channels, channels), 1)
    skip = jnp.sum(jnp.where(place == other, skip_ref[...], 0.0), axis=1, keepdims=True)
    direct_ref[...] = skip * gated
    if gathered_ref.shape[1] > tok_len:
        out_ref[...] = gathered_ref[:, tok_len:]
    else:
        out_ref[:channels] = own_ref[...]
        out_ref[channels:] = jnp.zeros_like(out_ref[channels:])
    for piece in range(PIECE):
        cut = slice(piece * LANES, (piece + 1) * LANES)
        for half in range(2):
            span = slice(half * channels, (half + 1) * channels)
            rows_ref[span, piece, :] = gated[:, cut]
            rows_ref[span, PIECE + piece, :] = filter_ref[:, cut]
    send_ref[...] = rows_ref[...].astype(jnp.bfloat16)


def convolve_kernel(
    recv_ref, fwd_hi, fwd_lo, back_hi, back_lo, in_hi, in_lo, out_hi, out_lo, twist_ref,
    send_ref, rows_ref, result_ref,
):
    rows_ref[...] = recv_ref[...].astype(jnp.float32)
    both = jnp.concatenate(
        [
            jnp.concatenate([rows_ref[:, piece, :], rows_ref[:, PIECE + piece, :]], axis=1)
            for piece in range(PIECE)
        ],
        axis=0,
    ).astype(jnp.bfloat16)
    cos_part = twist_ref[0]
    sin_part = twist_ref[1]
    outer = halves(lambda cut: dot(fwd_hi[cut], both) + dot(fwd_lo[cut], both), 2 * ROWS)
    real, imag = outer[:ROWS], outer[ROWS:]
    turned = []
    for cut in (slice(0, LANES), slice(LANES, 2 * LANES)):
        turned.append(
            jnp.concatenate(
                [
                    real[:, cut] * cos_part + imag[:, cut] * sin_part,
                    imag[:, cut] * cos_part - real[:, cut] * sin_part,
                ],
                axis=1,
            )
        )
    spectra = inner_transform(jnp.concatenate(turned, axis=0), in_hi, in_lo)
    source_real, source_imag = spectra[:ROWS, :LANES], spectra[:ROWS, LANES:]
    filter_real, filter_imag = spectra[ROWS:, :LANES], spectra[ROWS:, LANES:]
    product = jnp.concatenate(
        [
            source_real * filter_real - source_imag * filter_imag,
            source_real * filter_imag + source_imag * filter_real,
        ],
        axis=1,
    )
    inner = inner_transform(product, out_hi, out_lo)
    real, imag = inner[:, :LANES], inner[:, LANES:]
    upper, lower = split_value(
        jnp.concatenate(
            [real * cos_part - imag * sin_part, imag * cos_part + real * sin_part], axis=0
        )
    )
    half = 1 - lax.axis_index("context") % RING // (RING // 2)
    span = pl.ds(pl.multiple_of(half * (ROWS // 2), ROWS // 2), ROWS // 2)
    both = dot(back_hi[span, :], jnp.concatenate([upper, lower], axis=1))
    result = both[:, :LANES] + both[:, LANES:] + dot(back_lo[span, :], upper)
    for piece in range(PIECE):
        result_ref[:, piece, :] = result[piece * CHANNELS : (piece + 1) * CHANNELS]
    send_ref[...] = result_ref[...].astype(jnp.bfloat16)


def gate_kernel(recv_ref, gate_ref, direct_ref, out_ref, send_ref, rows_ref):
    channels, tok_len = gate_ref.shape
    rows_ref[...] = recv_ref[...].astype(jnp.float32)
    convolved = jnp.concatenate([rows_ref[:, piece, :] for piece in range(PIECE)], axis=1)
    out_gated = ((convolved + direct_ref[...]) * gate_ref[...]).astype(jnp.bfloat16)
    for copy in range(send_ref.shape[0]):
        send_ref[copy, :, :tok_len] = out_gated
        if send_ref.shape[2] > tok_len:
            send_ref[copy, :, tok_len:] = out_ref[:channels]


def mix_kernel(out_ref, gathered_ref, mixed_ref):
    tok_len = mixed_ref.shape[1]
    late = gathered_ref.shape[1] > tok_len
    mixed_ref[...] = lax.dot_general(
        gathered_ref[:, tok_len:] if late else out_ref[...],
        gathered_ref[:, :tok_len],
        (((0,), (0,)), ((), ())),
        preferred_element_type=jnp.float32,
    ).astype(jnp.bfloat16)


def near(*arrays):
    return [pltpu.with_memory_space_constraint(array, pltpu.VMEM) for array in arrays]


def far(*arrays):
    return [pltpu.with_memory_space_constraint(array, pltpu.HBM) for array in arrays]


def whole(count):
    return [pl.BlockSpec(memory_space=pltpu.VMEM) for _ in range(count)]


def shards(sequence, proj_in, conv_filter, skip_gain, proj_out):
    channels, tok_len = sequence.shape
    width = proj_out.shape[1]
    groups = lax.axis_size("tensor")
    ranks = lax.axis_size("context")

    early = lax.axis_index("context") % RING < RING // 2

    def begin(lanes):
        operands = [
            sequence,
            jnp.swapaxes(proj_in, 1, 2),
            conv_filter,
            skip_gain.reshape(1, channels),
            proj_out,
        ]
        send, *local = pl.pallas_call(
            spread_kernel,
            out_shape=(
                pltpu.VMEM((groups, channels, lanes), jnp.bfloat16),
                *[pltpu.VMEM(operand.shape, operand.dtype) for operand in operands[1:]],
            ),
            in_specs=whole(5),
            out_specs=tuple(whole(5)),
            name="spread",
        )(*far(*operands))
        gathered = lax.all_to_all(send, "tensor", 0, 0, axis_index_groups=[GROUP], tiled=True)
        return tuple(
            pl.pallas_call(
                project_kernel,
                out_shape=(
                    pltpu.VMEM((ranks, 2 * PIECE, LANES), jnp.bfloat16),
                    pltpu.VMEM((channels, tok_len), jnp.float32),
                    pltpu.VMEM((channels, tok_len), jnp.float32),
                    pltpu.VMEM((width, width), jnp.bfloat16),
                ),
                in_specs=whole(5),
                out_specs=tuple(whole(4)),
                scratch_shapes=[pltpu.VMEM((ranks, 2 * PIECE, LANES), jnp.float32)],
                compiler_params=pltpu.CompilerParams(vmem_limit_bytes=16 * 2**20),
                name="project",
            )(*near(gathered.reshape(width, lanes), *local))
        )

    send, gate, direct, proj_full = lax.cond(
        early, lambda: begin(tok_len + width), lambda: begin(tok_len)
    )

    recv = lax.all_to_all(send, "context", 0, 0, axis_index_groups=[ORDER], tiled=True)

    constants = [jnp.asarray(table) for table in tables()]
    send = pl.pallas_call(
        convolve_kernel,
        out_shape=pltpu.VMEM((channels, PIECE, LANES), jnp.bfloat16),
        in_specs=whole(1 + len(constants)),
        out_specs=whole(1)[0],
        scratch_shapes=[
            pltpu.VMEM((ranks, 2 * PIECE, LANES), jnp.float32),
            pltpu.VMEM((channels, PIECE, LANES), jnp.float32),
        ],
        compiler_params=pltpu.CompilerParams(vmem_limit_bytes=24 * 2**20),
        name="convolve",
    )(recv, *constants)

    recv = lax.all_to_all(send, "context", 0, 0, axis_index_groups=HALVES, tiled=True)

    def finish(lanes):
        send = pl.pallas_call(
            gate_kernel,
            out_shape=pltpu.VMEM((groups, channels, lanes), jnp.bfloat16),
            in_specs=whole(4),
            out_specs=whole(1)[0],
            scratch_shapes=[pltpu.VMEM((channels, PIECE, LANES), jnp.float32)],
            compiler_params=pltpu.CompilerParams(vmem_limit_bytes=16 * 2**20),
            name="gate",
        )(*near(recv, gate, direct, proj_full))
        gathered = lax.all_to_all(send, "tensor", 0, 0, axis_index_groups=[GROUP], tiled=True)
        return pl.pallas_call(
            mix_kernel,
            out_shape=pltpu.HBM((width, tok_len), jnp.bfloat16),
            in_specs=whole(2),
            out_specs=whole(1)[0],
            compiler_params=pltpu.CompilerParams(vmem_limit_bytes=16 * 2**20),
            name="mix",
        )(*near(proj_full, gathered.reshape(width, lanes)))

    return lax.cond(early, lambda: finish(tok_len), lambda: finish(tok_len + width))


def solution(mesh):
    return jax.shard_map(
        shards,
        mesh=mesh,
        in_specs=(
            P("tensor", "context"),
            P(None, None, "tensor"),
            P("tensor", "context"),
            P("tensor"),
            P("tensor", None),
        ),
        out_specs=P(None, "context"),
        check_vma=False,
    )
```

```python
import math

import jax
import jax.numpy as jnp
import numpy as np
from jax import lax
from jax.experimental import pallas as pl
from jax.experimental.pallas import tpu as pltpu
from jax.sharding import PartitionSpec as P

ROWS = 256
LANES = 128
LENGTH = ROWS * LANES
PIECE = 4
RANKS = ROWS // PIECE
LINES, RING = 4, 16
CHANNELS = RANKS // 2

TURN = 2
HALVES = [
    [(outer + TURN) % LINES * RING + inner for outer in range(LINES) for inner in ring]
    for ring in ((10, 11, 12, 13, 14, 15, 8, 9), (6, 7, 5, 4, 3, 2, 1, 0))
]
ORDER = HALVES[0] + HALVES[1]

GROUP = [5, 4, 6, 7, 0, 1, 2, 3]


def split_table(table):
    upper = table.astype(jnp.bfloat16)
    lower = (table - upper.astype(np.float64)).astype(jnp.bfloat16)
    return upper, lower


def tables():
    come = np.concatenate([np.asarray(ORDER) * PIECE + piece for piece in range(PIECE)])
    go = np.concatenate(
        [np.asarray(half) * PIECE + piece for half in HALVES for piece in range(PIECE)]
    )
    low = np.arange(ROWS)
    lane = np.arange(LANES)

    def outer(row):
        turn = 2.0 * np.pi * np.outer(low + 0.25, row) / ROWS
        return np.concatenate([np.cos(turn), -np.sin(turn)], axis=0)

    turn = 2.0 * np.pi * np.outer(low + 0.25, lane) / LENGTH
    twist = np.stack([np.cos(turn), np.sin(turn)]).astype(np.float32)
    turn = 2.0 * np.pi * (np.outer(lane, lane) % LANES) / LANES
    cos_part, sin_part = np.cos(turn), np.sin(turn)
    inner = np.block([[cos_part, -sin_part], [sin_part, cos_part]])
    return (
        *split_table(outer(come)),
        *split_table(outer(go).T / LENGTH),
        *split_table(inner),
        *split_table(inner.T),
        twist,
    )


def dot(left, right):
    return jnp.dot(left, right, preferred_element_type=jnp.float32)


def split_value(value):
    upper = value.astype(jnp.bfloat16)
    lower = (value - upper.astype(jnp.float32)).astype(jnp.bfloat16)
    return upper, lower


def halves(part, rows):
    middle = rows // 2
    return jnp.concatenate([part(slice(0, middle)), part(slice(middle, rows))], axis=0)


def inner_transform(value, table_hi, table_lo):
    upper, lower = split_value(value)
    return halves(
        lambda cut: dot(upper[cut], table_hi[...])
        + dot(lower[cut], table_hi[...])
        + dot(upper[cut], table_lo[...]),
        value.shape[0],
    )


def spread_kernel(
    sequence_ref, proj_ref, filter_ref, skip_ref, out_ref,
    send_ref, proj_copy, filter_copy, skip_copy, out_copy,
):
    tok_len = sequence_ref.shape[1]
    for copy in range(send_ref.shape[0]):
        send_ref[copy, :, :tok_len] = sequence_ref[...]
        if send_ref.shape[2] > tok_len:
            send_ref[copy, :, tok_len:] = out_ref[...]
    proj_copy[...] = proj_ref[...]
    filter_copy[...] = filter_ref[...]
    skip_copy[...] = skip_ref[...]
    out_copy[...] = out_ref[...]


def project_kernel(
    gathered_ref, proj_ref, filter_ref, skip_ref, own_ref,
    send_ref, gate_ref, direct_ref, out_ref, rows_ref,
):
    channels, tok_len = filter_ref.shape
    sequence = jnp.concatenate(
        [
            gathered_ref[place * channels : (place + 1) * channels, :tok_len]
            for place in np.argsort(GROUP).tolist()
        ],
        axis=0,
    )
    first, gate, value = [dot(proj_ref[index], sequence) for index in range(3)]
    gated = value * first
    gate_ref[...] = gate
    place = lax.broadcasted_iota(jnp.int32, (channels, channels), 0)
    other = lax.broadcasted_iota(jnp.int32, (channels, channels), 1)
    skip = jnp.sum(jnp.where(place == other, skip_ref[...], 0.0), axis=1, keepdims=True)
    direct_ref[...] = skip * gated
    if gathered_ref.shape[1] > tok_len:
        out_ref[...] = gathered_ref[:, tok_len:]
    else:
        out_ref[:channels] = own_ref[...]
        out_ref[channels:] = jnp.zeros_like(out_ref[channels:])
    for piece in range(PIECE):
        cut = slice(piece * LANES, (piece + 1) * LANES)
        for half in range(2):
            span = slice(half * channels, (half + 1) * channels)
            rows_ref[span, piece, :] = gated[:, cut]
            rows_ref[span, PIECE + piece, :] = filter_ref[:, cut]
    send_ref[...] = rows_ref[...].astype(jnp.bfloat16)


def convolve_kernel(
    recv_ref, fwd_hi, fwd_lo, back_hi, back_lo, in_hi, in_lo, out_hi, out_lo, twist_ref,
    send_ref, rows_ref, result_ref,
):
    rows_ref[...] = recv_ref[...].astype(jnp.float32)
    both = jnp.concatenate(
        [
            jnp.concatenate([rows_ref[:, piece, :], rows_ref[:, PIECE + piece, :]], axis=1)
            for piece in range(PIECE)
        ],
        axis=0,
    ).astype(jnp.bfloat16)
    cos_part = twist_ref[0]
    sin_part = twist_ref[1]
    outer = halves(lambda cut: dot(fwd_hi[cut], both) + dot(fwd_lo[cut], both), 2 * ROWS)
    real, imag = outer[:ROWS], outer[ROWS:]
    turned = []
    for cut in (slice(0, LANES), slice(LANES, 2 * LANES)):
        turned.append(
            jnp.concatenate(
                [
                    real[:, cut] * cos_part + imag[:, cut] * sin_part,
                    imag[:, cut] * cos_part - real[:, cut] * sin_part,
                ],
                axis=1,
            )
        )
    spectra = inner_transform(jnp.concatenate(turned, axis=0), in_hi, in_lo)
    source_real, source_imag = spectra[:ROWS, :LANES], spectra[:ROWS, LANES:]
    filter_real, filter_imag = spectra[ROWS:, :LANES], spectra[ROWS:, LANES:]
    product = jnp.concatenate(
        [
            source_real * filter_real - source_imag * filter_imag,
            source_real * filter_imag + source_imag * filter_real,
        ],
        axis=1,
    )
    inner = inner_transform(product, out_hi, out_lo)
    real, imag = inner[:, :LANES], inner[:, LANES:]
    upper, lower = split_value(
        jnp.concatenate(
            [real * cos_part - imag * sin_part, imag * cos_part + real * sin_part], axis=0
        )
    )
    half = 1 - lax.axis_index("context") % RING // (RING // 2)
    span = pl.ds(pl.multiple_of(half * (ROWS // 2), ROWS // 2), ROWS // 2)
    both = dot(back_hi[span, :], jnp.concatenate([upper, lower], axis=1))
    result = both[:, :LANES] + both[:, LANES:] + dot(back_lo[span, :], upper)
    for piece in range(PIECE):
        result_ref[:, piece, :] = result[piece * CHANNELS : (piece + 1) * CHANNELS]
    send_ref[...] = result_ref[...].astype(jnp.bfloat16)


def gate_kernel(recv_ref, gate_ref, direct_ref, out_ref, send_ref, rows_ref):
    channels, tok_len = gate_ref.shape
    rows_ref[...] = recv_ref[...].astype(jnp.float32)
    convolved = jnp.concatenate([rows_ref[:, piece, :] for piece in range(PIECE)], axis=1)
    out_gated = ((convolved + direct_ref[...]) * gate_ref[...]).astype(jnp.bfloat16)
    for copy in range(send_ref.shape[0]):
        send_ref[copy, :, :tok_len] = out_gated
        if send_ref.shape[2] > tok_len:
            send_ref[copy, :, tok_len:] = out_ref[:channels]


def mix_kernel(out_ref, gathered_ref, mixed_ref):
    tok_len = mixed_ref.shape[1]
    late = gathered_ref.shape[1] > tok_len
    mixed_ref[...] = lax.dot_general(
        gathered_ref[:, tok_len:] if late else out_ref[...],
        gathered_ref[:, :tok_len],
        (((0,), (0,)), ((), ())),
        preferred_element_type=jnp.float32,
    ).astype(jnp.bfloat16)


def near(*arrays):
    return [pltpu.with_memory_space_constraint(array, pltpu.VMEM) for array in arrays]


def far(*arrays):
    return [pltpu.with_memory_space_constraint(array, pltpu.HBM) for array in arrays]


def whole(count):
    return [pl.BlockSpec(memory_space=pltpu.VMEM) for _ in range(count)]


def shards(sequence, proj_in, conv_filter, skip_gain, proj_out):
    channels, tok_len = sequence.shape
    width = proj_out.shape[1]
    groups = lax.axis_size("tensor")
    ranks = lax.axis_size("context")

    early = lax.axis_index("context") % RING < RING // 2

    def begin(lanes):
        operands = [
            sequence,
            jnp.swapaxes(proj_in, 1, 2),
            conv_filter,
            skip_gain.reshape(1, channels),
            proj_out,
        ]
        send, *local = pl.pallas_call(
            spread_kernel,
            out_shape=(
                pltpu.VMEM((groups, channels, lanes), jnp.bfloat16),
                *[pltpu.VMEM(operand.shape, operand.dtype) for operand in operands[1:]],
            ),
            in_specs=whole(5),
            out_specs=tuple(whole(5)),
            name="spread",
        )(*far(*operands))
        gathered = lax.all_to_all(send, "tensor", 0, 0, axis_index_groups=[GROUP], tiled=True)
        return tuple(
            pl.pallas_call(
                project_kernel,
                out_shape=(
                    pltpu.VMEM((ranks, 2 * PIECE, LANES), jnp.bfloat16),
                    pltpu.VMEM((channels, tok_len), jnp.float32),
                    pltpu.VMEM((channels, tok_len), jnp.float32),
                    pltpu.VMEM((width, width), jnp.bfloat16),
                ),
                in_specs=whole(5),
                out_specs=tuple(whole(4)),
                scratch_shapes=[pltpu.VMEM((ranks, 2 * PIECE, LANES), jnp.float32)],
                compiler_params=pltpu.CompilerParams(vmem_limit_bytes=16 * 2**20),
                name="project",
            )(*near(gathered.reshape(width, lanes), *local))
        )

    send, gate, direct, proj_full = lax.cond(
        early, lambda: begin(tok_len + width), lambda: begin(tok_len)
    )

    recv = lax.all_to_all(send, "context", 0, 0, axis_index_groups=[ORDER], tiled=True)

    constants = [jnp.asarray(table) for table in tables()]
    send = pl.pallas_call(
        convolve_kernel,
        out_shape=pltpu.VMEM((channels, PIECE, LANES), jnp.bfloat16),
        in_specs=whole(1 + len(constants)),
        out_specs=whole(1)[0],
        scratch_shapes=[
            pltpu.VMEM((ranks, 2 * PIECE, LANES), jnp.float32),
            pltpu.VMEM((channels, PIECE, LANES), jnp.float32),
        ],
        compiler_params=pltpu.CompilerParams(vmem_limit_bytes=24 * 2**20),
        name="convolve",
    )(recv, *constants)

    recv = lax.all_to_all(send, "context", 0, 0, axis_index_groups=HALVES, tiled=True)

    def finish(lanes):
        send = pl.pallas_call(
            gate_kernel,
            out_shape=pltpu.VMEM((groups, channels, lanes), jnp.bfloat16),
            in_specs=whole(4),
            out_specs=whole(1)[0],
            scratch_shapes=[pltpu.VMEM((channels, PIECE, LANES), jnp.float32)],
            compiler_params=pltpu.CompilerParams(vmem_limit_bytes=16 * 2**20),
            name="gate",
        )(*near(recv, gate, direct, proj_full))
        gathered = lax.all_to_all(send, "tensor", 0, 0, axis_index_groups=[GROUP], tiled=True)
        return pl.pallas_call(
            mix_kernel,
            out_shape=pltpu.HBM((width, tok_len), jnp.bfloat16),
            in_specs=whole(2),
            out_specs=whole(1)[0],
            compiler_params=pltpu.CompilerParams(vmem_limit_bytes=16 * 2**20),
            name="mix",
        )(*near(proj_full, gathered.reshape(width, lanes)))

    return lax.cond(early, lambda: finish(tok_len), lambda: finish(tok_len + width))


def solution(mesh):
    return jax.shard_map(
        shards,
        mesh=mesh,
        in_specs=(
            P("tensor", "context"),
            P(None, None, "tensor"),
            P("tensor", "context"),
            P("tensor"),
            P("tensor", None),
        ),
        out_specs=P(None, "context"),
        check_vma=False,
    )
```

```python
import math

import jax
import jax.numpy as jnp
import numpy as np
from jax import lax
from jax.experimental import pallas as pl
from jax.experimental.pallas import tpu as pltpu
from jax.sharding import PartitionSpec as P

ROWS = 256
LANES = 128
LENGTH = ROWS * LANES
PIECE = 4
RANKS = ROWS // PIECE
LINES, RING = 4, 16
CHANNELS = RANKS // 2

TURN = 2
HALVES = [
    [(outer + TURN) % LINES * RING + inner for outer in range(LINES) for inner in ring]
    for ring in ((11, 12, 13, 14, 15, 8, 9, 10), (6, 7, 5, 4, 3, 2, 1, 0))
]
ORDER = HALVES[0] + HALVES[1]

EARLY = 3

GROUP = [5, 4, 6, 7, 0, 1, 2, 3]


def split_table(table):
    upper = table.astype(jnp.bfloat16)
    lower = (table - upper.astype(np.float64)).astype(jnp.bfloat16)
    return upper, lower


def tables():
    come = np.concatenate([np.asarray(ORDER) * PIECE + piece for piece in range(PIECE)])
    go = np.concatenate(
        [np.asarray(half) * PIECE + piece for half in HALVES for piece in range(PIECE)]
    )
    low = np.arange(ROWS)
    lane = np.arange(LANES)

    def outer(row):
        turn = 2.0 * np.pi * np.outer(low + 0.25, row) / ROWS
        return np.concatenate([np.cos(turn), -np.sin(turn)], axis=0)

    turn = 2.0 * np.pi * np.outer(low + 0.25, lane) / LENGTH
    twist = np.stack([np.cos(turn), np.sin(turn)]).astype(np.float32)
    turn = 2.0 * np.pi * (np.outer(lane, lane) % LANES) / LANES
    cos_part, sin_part = np.cos(turn), np.sin(turn)
    inner = np.block([[cos_part, -sin_part], [sin_part, cos_part]])
    return (
        *split_table(outer(come)),
        *split_table(outer(go).T / LENGTH),
        *split_table(inner),
        *split_table(inner.T),
        twist,
    )


def dot(left, right):
    return jnp.dot(left, right, preferred_element_type=jnp.float32)


def split_value(value):
    upper = value.astype(jnp.bfloat16)
    lower = (value - upper.astype(jnp.float32)).astype(jnp.bfloat16)
    return upper, lower


def halves(part, rows):
    middle = rows // 2
    return jnp.concatenate([part(slice(0, middle)), part(slice(middle, rows))], axis=0)


def inner_transform(value, table_hi, table_lo):
    upper, lower = split_value(value)
    return halves(
        lambda cut: dot(upper[cut], table_hi[...])
        + dot(lower[cut], table_hi[...])
        + dot(upper[cut], table_lo[...]),
        value.shape[0],
    )


def spread_kernel(
    sequence_ref, proj_ref, filter_ref, skip_ref, out_ref,
    send_ref, proj_copy, filter_copy, skip_copy, out_copy,
):
    tok_len = sequence_ref.shape[1]
    for copy in range(send_ref.shape[0]):
        send_ref[copy, :, :tok_len] = sequence_ref[...]
        if send_ref.shape[2] > tok_len:
            send_ref[copy, :, tok_len:] = out_ref[...]
    proj_copy[...] = proj_ref[...]
    filter_copy[...] = filter_ref[...]
    skip_copy[...] = skip_ref[...]
    out_copy[...] = out_ref[...]


def project_kernel(
    gathered_ref, proj_ref, filter_ref, skip_ref, own_ref,
    send_ref, gate_ref, direct_ref, out_ref, rows_ref,
):
    channels, tok_len = filter_ref.shape
    sequence = jnp.concatenate(
        [
            gathered_ref[place * channels : (place + 1) * channels, :tok_len]
            for place in np.argsort(GROUP).tolist()
        ],
        axis=0,
    )
    first, gate, value = [dot(proj_ref[index], sequence) for index in range(3)]
    gated = value * first
    gate_ref[...] = gate
    place = lax.broadcasted_iota(jnp.int32, (channels, channels), 0)
    other = lax.broadcasted_iota(jnp.int32, (channels, channels), 1)
    skip = jnp.sum(jnp.where(place == other, skip_ref[...], 0.0), axis=1, keepdims=True)
    direct_ref[...] = skip * gated
    if gathered_ref.shape[1] > tok_len:
        out_ref[...] = gathered_ref[:, tok_len:]
    else:
        out_ref[:channels] = own_ref[...]
        out_ref[channels:] = jnp.zeros_like(out_ref[channels:])
    for piece in range(PIECE):
        cut = slice(piece * LANES, (piece + 1) * LANES)
        for half in range(2):
            span = slice(half * channels, (half + 1) * channels)
            rows_ref[span, piece, :] = gated[:, cut]
            rows_ref[span, PIECE + piece, :] = filter_ref[:, cut]
    send_ref[...] = rows_ref[...].astype(jnp.bfloat16)


def convolve_kernel(
    recv_ref, fwd_hi, fwd_lo, back_hi, back_lo, in_hi, in_lo, out_hi, out_lo, twist_ref,
    send_ref, rows_ref, result_ref,
):
    rows_ref[...] = recv_ref[...].astype(jnp.float32)
    both = jnp.concatenate(
        [
            jnp.concatenate([rows_ref[:, piece, :], rows_ref[:, PIECE + piece, :]], axis=1)
            for piece in range(PIECE)
        ],
        axis=0,
    ).astype(jnp.bfloat16)
    cos_part = twist_ref[0]
    sin_part = twist_ref[1]
    outer = halves(lambda cut: dot(fwd_hi[cut], both) + dot(fwd_lo[cut], both), 2 * ROWS)
    real, imag = outer[:ROWS], outer[ROWS:]
    turned = []
    for cut in (slice(0, LANES), slice(LANES, 2 * LANES)):
        turned.append(
            jnp.concatenate(
                [
                    real[:, cut] * cos_part + imag[:, cut] * sin_part,
                    imag[:, cut] * cos_part - real[:, cut] * sin_part,
                ],
                axis=1,
            )
        )
    spectra = inner_transform(jnp.concatenate(turned, axis=0), in_hi, in_lo)
    source_real, source_imag = spectra[:ROWS, :LANES], spectra[:ROWS, LANES:]
    filter_real, filter_imag = spectra[ROWS:, :LANES], spectra[ROWS:, LANES:]
    product = jnp.concatenate(
        [
            source_real * filter_real - source_imag * filter_imag,
            source_real * filter_imag + source_imag * filter_real,
        ],
        axis=1,
    )
    inner = inner_transform(product, out_hi, out_lo)
    real, imag = inner[:, :LANES], inner[:, LANES:]
    upper, lower = split_value(
        jnp.concatenate(
            [real * cos_part - imag * sin_part, imag * cos_part + real * sin_part], axis=0
        )
    )
    half = 1 - lax.axis_index("context") % RING // (RING // 2)
    span = pl.ds(pl.multiple_of(half * (ROWS // 2), ROWS // 2), ROWS // 2)
    both = dot(back_hi[span, :], jnp.concatenate([upper, lower], axis=1))
    result = both[:, :LANES] + both[:, LANES:] + dot(back_lo[span, :], upper)
    for piece in range(PIECE):
        result_ref[:, piece, :] = result[piece * CHANNELS : (piece + 1) * CHANNELS]
    send_ref[...] = result_ref[...].astype(jnp.bfloat16)


def gate_kernel(recv_ref, gate_ref, direct_ref, out_ref, send_ref, rows_ref):
    channels, tok_len = gate_ref.shape
    rows_ref[...] = recv_ref[...].astype(jnp.float32)
    convolved = jnp.concatenate([rows_ref[:, piece, :] for piece in range(PIECE)], axis=1)
    out_gated = ((convolved + direct_ref[...]) * gate_ref[...]).astype(jnp.bfloat16)
    for copy in range(send_ref.shape[0]):
        send_ref[copy, :, :tok_len] = out_gated
        if send_ref.shape[2] > tok_len:
            send_ref[copy, :, tok_len:] = out_ref[:channels]


def mix_kernel(out_ref, gathered_ref, mixed_ref):
    tok_len = mixed_ref.shape[1]
    late = gathered_ref.shape[1] > tok_len
    mixed_ref[...] = lax.dot_general(
        gathered_ref[:, tok_len:] if late else out_ref[...],
        gathered_ref[:, :tok_len],
        (((0,), (0,)), ((), ())),
        preferred_element_type=jnp.float32,
    ).astype(jnp.bfloat16)


def near(*arrays):
    return [pltpu.with_memory_space_constraint(array, pltpu.VMEM) for array in arrays]


def far(*arrays):
    return [pltpu.with_memory_space_constraint(array, pltpu.HBM) for array in arrays]


def whole(count):
    return [pl.BlockSpec(memory_space=pltpu.VMEM) for _ in range(count)]


def shards(sequence, proj_in, conv_filter, skip_gain, proj_out):
    channels, tok_len = sequence.shape
    width = proj_out.shape[1]
    groups = lax.axis_size("tensor")
    ranks = lax.axis_size("context")

    early = lax.axis_index("context") % RING < EARLY

    def begin(lanes):
        operands = [
            sequence,
            jnp.swapaxes(proj_in, 1, 2),
            conv_filter,
            skip_gain.reshape(1, channels),
            proj_out,
        ]
        send, *local = pl.pallas_call(
            spread_kernel,
            out_shape=(
                pltpu.VMEM((groups, channels, lanes), jnp.bfloat16),
                *[pltpu.VMEM(operand.shape, operand.dtype) for operand in operands[1:]],
            ),
            in_specs=whole(5),
            out_specs=tuple(whole(5)),
            name="spread",
        )(*far(*operands))
        gathered = lax.all_to_all(send, "tensor", 0, 0, axis_index_groups=[GROUP], tiled=True)
        return tuple(
            pl.pallas_call(
                project_kernel,
                out_shape=(
                    pltpu.VMEM((ranks, 2 * PIECE, LANES), jnp.bfloat16),
                    pltpu.VMEM((channels, tok_len), jnp.float32),
                    pltpu.VMEM((channels, tok_len), jnp.float32),
                    pltpu.VMEM((width, width), jnp.bfloat16),
                ),
                in_specs=whole(5),
                out_specs=tuple(whole(4)),
                scratch_shapes=[pltpu.VMEM((ranks, 2 * PIECE, LANES), jnp.float32)],
                compiler_params=pltpu.CompilerParams(vmem_limit_bytes=16 * 2**20),
                name="project",
            )(*near(gathered.reshape(width, lanes), *local))
        )

    send, gate, direct, proj_full = lax.cond(
        early, lambda: begin(tok_len + width), lambda: begin(tok_len)
    )

    recv = lax.all_to_all(send, "context", 0, 0, axis_index_groups=[ORDER], tiled=True)

    constants = [jnp.asarray(table) for table in tables()]
    send = pl.pallas_call(
        convolve_kernel,
        out_shape=pltpu.VMEM((channels, PIECE, LANES), jnp.bfloat16),
        in_specs=whole(1 + len(constants)),
        out_specs=whole(1)[0],
        scratch_shapes=[
            pltpu.VMEM((ranks, 2 * PIECE, LANES), jnp.float32),
            pltpu.VMEM((channels, PIECE, LANES), jnp.float32),
        ],
        compiler_params=pltpu.CompilerParams(vmem_limit_bytes=24 * 2**20),
        name="convolve",
    )(recv, *constants)

    recv = lax.all_to_all(send, "context", 0, 0, axis_index_groups=HALVES, tiled=True)

    def finish(lanes):
        send = pl.pallas_call(
            gate_kernel,
            out_shape=pltpu.VMEM((groups, channels, lanes), jnp.bfloat16),
            in_specs=whole(4),
            out_specs=whole(1)[0],
            scratch_shapes=[pltpu.VMEM((channels, PIECE, LANES), jnp.float32)],
            compiler_params=pltpu.CompilerParams(vmem_limit_bytes=16 * 2**20),
            name="gate",
        )(*near(recv, gate, direct, proj_full))
        gathered = lax.all_to_all(send, "tensor", 0, 0, axis_index_groups=[GROUP], tiled=True)
        return pl.pallas_call(
            mix_kernel,
            out_shape=pltpu.HBM((width, tok_len), jnp.bfloat16),
            in_specs=whole(2),
            out_specs=whole(1)[0],
            compiler_params=pltpu.CompilerParams(vmem_limit_bytes=16 * 2**20),
            name="mix",
        )(*near(proj_full, gathered.reshape(width, lanes)))

    return lax.cond(early, lambda: finish(tok_len), lambda: finish(tok_len + width))


def solution(mesh):
    return jax.shard_map(
        shards,
        mesh=mesh,
        in_specs=(
            P("tensor", "context"),
            P(None, None, "tensor"),
            P("tensor", "context"),
            P("tensor"),
            P("tensor", None),
        ),
        out_specs=P(None, "context"),
        check_vma=False,
    )
```

```python
import math

import jax
import jax.numpy as jnp
import numpy as np
from jax import lax
from jax.experimental import pallas as pl
from jax.experimental.pallas import tpu as pltpu
from jax.sharding import PartitionSpec as P

ROWS = 256
LANES = 128
LENGTH = ROWS * LANES
PIECE = 4
RANKS = ROWS // PIECE
LINES, RING = 4, 16
CHANNELS = RANKS // 2

TURN = 2
HALVES = [
    [(outer + TURN) % LINES * RING + inner for outer in range(LINES) for inner in ring]
    for ring in ((10, 11, 12, 13, 14, 15, 8, 9), (6, 7, 5, 4, 3, 2, 1, 0))
]
ORDER = HALVES[0] + HALVES[1]

GROUP = [5, 4, 6, 7, 0, 1, 2, 3]


def split_table(table):
    upper = table.astype(jnp.bfloat16)
    lower = (table - upper.astype(np.float64)).astype(jnp.bfloat16)
    return upper, lower


def tables():
    come = np.concatenate([np.asarray(ORDER) * PIECE + piece for piece in range(PIECE)])
    go = np.concatenate(
        [np.asarray(half) * PIECE + piece for half in HALVES for piece in range(PIECE)]
    )
    low = np.arange(ROWS)
    lane = np.arange(LANES)

    def outer(row):
        turn = 2.0 * np.pi * np.outer(low + 0.25, row) / ROWS
        return np.concatenate([np.cos(turn), -np.sin(turn)], axis=0)

    turn = 2.0 * np.pi * np.outer(low + 0.25, lane) / LENGTH
    twist = np.stack([np.cos(turn), np.sin(turn)]).astype(np.float32)
    turn = 2.0 * np.pi * (np.outer(lane, lane) % LANES) / LANES
    cos_part, sin_part = np.cos(turn), np.sin(turn)
    inner = np.block([[cos_part, -sin_part], [sin_part, cos_part]])
    return (
        *split_table(outer(come)),
        *split_table(outer(go).T / LENGTH),
        *split_table(inner),
        *split_table(inner.T),
        twist,
    )


def dot(left, right):
    return jnp.dot(left, right, preferred_element_type=jnp.float32)


def split_value(value):
    upper = value.astype(jnp.bfloat16)
    lower = (value - upper.astype(jnp.float32)).astype(jnp.bfloat16)
    return upper, lower


def halves(part, rows):
    middle = rows // 2
    return jnp.concatenate([part(slice(0, middle)), part(slice(middle, rows))], axis=0)


def inner_transform(value, table_hi, table_lo):
    upper, lower = split_value(value)
    return halves(
        lambda cut: dot(upper[cut], table_hi[...])
        + dot(lower[cut], table_hi[...])
        + dot(upper[cut], table_lo[...]),
        value.shape[0],
    )


def spread_kernel(
    sequence_ref, proj_ref, filter_ref, skip_ref, out_ref,
    send_ref, proj_copy, filter_copy, skip_copy, out_copy,
):
    tok_len = sequence_ref.shape[1]
    for copy in range(send_ref.shape[0]):
        send_ref[copy, :, :tok_len] = sequence_ref[...]
        if send_ref.shape[2] > tok_len:
            send_ref[copy, :, tok_len:] = out_ref[...]
    proj_copy[...] = proj_ref[...]
    filter_copy[...] = filter_ref[...]
    skip_copy[...] = skip_ref[...]
    out_copy[...] = out_ref[...]


def project_kernel(
    gathered_ref, proj_ref, filter_ref, skip_ref, own_ref,
    send_ref, gate_ref, direct_ref, out_ref, rows_ref,
):
    channels, tok_len = filter_ref.shape
    sequence = jnp.concatenate(
        [
            gathered_ref[place * channels : (place + 1) * channels, :tok_len]
            for place in np.argsort(GROUP).tolist()
        ],
        axis=0,
    )
    first, gate, value = [dot(proj_ref[index], sequence) for index in range(3)]
    gated = value * first
    gate_ref[...] = gate
    place = lax.broadcasted_iota(jnp.int32, (channels, channels), 0)
    other = lax.broadcasted_iota(jnp.int32, (channels, channels), 1)
    skip = jnp.sum(jnp.where(place == other, skip_ref[...], 0.0), axis=1, keepdims=True)
    direct_ref[...] = skip * gated
    if gathered_ref.shape[1] > tok_len:
        out_ref[...] = gathered_ref[:, tok_len:]
    else:
        out_ref[:channels] = own_ref[...]
    for piece in range(PIECE):
        cut = slice(piece * LANES, (piece + 1) * LANES)
        rows_ref[:, piece, :] = gated[:, cut]
        rows_ref[:, PIECE + piece, :] = filter_ref[:, cut]
    rows = rows_ref[...].astype(jnp.bfloat16)
    for half in range(2):
        send_ref[half * channels : (half + 1) * channels] = rows


def convolve_kernel(
    recv_ref, fwd_hi, fwd_lo, back_hi, back_lo, in_hi, in_lo, out_hi, out_lo, twist_ref,
    send_ref, rows_ref, result_ref,
):
    rows_ref[...] = recv_ref[...].astype(jnp.float32)
    both = jnp.concatenate(
        [
            jnp.concatenate([rows_ref[:, piece, :], rows_ref[:, PIECE + piece, :]], axis=1)
            for piece in range(PIECE)
        ],
        axis=0,
    ).astype(jnp.bfloat16)
    cos_part = twist_ref[0]
    sin_part = twist_ref[1]
    outer = halves(lambda cut: dot(fwd_hi[cut], both) + dot(fwd_lo[cut], both), 2 * ROWS)
    real, imag = outer[:ROWS], outer[ROWS:]
    turned = []
    for cut in (slice(0, LANES), slice(LANES, 2 * LANES)):
        turned.append(
            jnp.concatenate(
                [
                    real[:, cut] * cos_part + imag[:, cut] * sin_part,
                    imag[:, cut] * cos_part - real[:, cut] * sin_part,
                ],
                axis=1,
            )
        )
    spectra = inner_transform(jnp.concatenate(turned, axis=0), in_hi, in_lo)
    source_real, source_imag = spectra[:ROWS, :LANES], spectra[:ROWS, LANES:]
    filter_real, filter_imag = spectra[ROWS:, :LANES], spectra[ROWS:, LANES:]
    product = jnp.concatenate(
        [
            source_real * filter_real - source_imag * filter_imag,
            source_real * filter_imag + source_imag * filter_real,
        ],
        axis=1,
    )
    inner = inner_transform(product, out_hi, out_lo)
    real, imag = inner[:, :LANES], inner[:, LANES:]
    upper, lower = split_value(
        jnp.concatenate(
            [real * cos_part - imag * sin_part, imag * cos_part + real * sin_part], axis=0
        )
    )
    half = 1 - lax.axis_index("context") % RING // (RING // 2)
    span = pl.ds(pl.multiple_of(half * (ROWS // 2), ROWS // 2), ROWS // 2)
    both = dot(back_hi[span, :], jnp.concatenate([upper, lower], axis=1))
    result = both[:, :LANES] + both[:, LANES:] + dot(back_lo[span, :], upper)
    for piece in range(PIECE):
        result_ref[:, piece, :] = result[piece * CHANNELS : (piece + 1) * CHANNELS]
    send_ref[...] = result_ref[...].astype(jnp.bfloat16)


def gate_kernel(recv_ref, gate_ref, direct_ref, out_ref, send_ref, rows_ref):
    channels, tok_len = gate_ref.shape
    rows_ref[...] = recv_ref[...].astype(jnp.float32)
    convolved = jnp.concatenate([rows_ref[:, piece, :] for piece in range(PIECE)], axis=1)
    out_gated = ((convolved + direct_ref[...]) * gate_ref[...]).astype(jnp.bfloat16)
    for copy in range(send_ref.shape[0]):
        send_ref[copy, :, :tok_len] = out_gated
        if send_ref.shape[2] > tok_len:
            send_ref[copy, :, tok_len:] = out_ref[:channels]


def mix_kernel(out_ref, gathered_ref, mixed_ref):
    tok_len = mixed_ref.shape[1]
    late = gathered_ref.shape[1] > tok_len
    mixed_ref[...] = lax.dot_general(
        gathered_ref[:, tok_len:] if late else out_ref[...],
        gathered_ref[:, :tok_len],
        (((0,), (0,)), ((), ())),
        preferred_element_type=jnp.float32,
    ).astype(jnp.bfloat16)


def near(*arrays):
    return [pltpu.with_memory_space_constraint(array, pltpu.VMEM) for array in arrays]


def far(*arrays):
    return [pltpu.with_memory_space_constraint(array, pltpu.HBM) for array in arrays]


def whole(count):
    return [pl.BlockSpec(memory_space=pltpu.VMEM) for _ in range(count)]


def shards(sequence, proj_in, conv_filter, skip_gain, proj_out):
    channels, tok_len = sequence.shape
    width = proj_out.shape[1]
    groups = lax.axis_size("tensor")
    ranks = lax.axis_size("context")

    early = lax.axis_index("context") % RING < RING // 2

    def begin(lanes):
        operands = [
            sequence,
            jnp.swapaxes(proj_in, 1, 2),
            conv_filter,
            skip_gain.reshape(1, channels),
            proj_out,
        ]
        send, *local = pl.pallas_call(
            spread_kernel,
            out_shape=(
                pltpu.VMEM((groups, channels, lanes), jnp.bfloat16),
                *[pltpu.VMEM(operand.shape, operand.dtype) for operand in operands[1:]],
            ),
            in_specs=whole(5),
            out_specs=tuple(whole(5)),
            name="spread",
        )(*far(*operands))
        gathered = lax.all_to_all(send, "tensor", 0, 0, axis_index_groups=[GROUP], tiled=True)
        return tuple(
            pl.pallas_call(
                project_kernel,
                out_shape=(
                    pltpu.VMEM((ranks, 2 * PIECE, LANES), jnp.bfloat16),
                    pltpu.VMEM((channels, tok_len), jnp.float32),
                    pltpu.VMEM((channels, tok_len), jnp.float32),
                    pltpu.VMEM((width, width), jnp.bfloat16),
                ),
                in_specs=whole(5),
                out_specs=tuple(whole(4)),
                scratch_shapes=[pltpu.VMEM((channels, 2 * PIECE, LANES), jnp.float32)],
                compiler_params=pltpu.CompilerParams(vmem_limit_bytes=16 * 2**20),
                name="project",
            )(*near(gathered.reshape(width, lanes), *local))
        )

    send, gate, direct, proj_full = lax.cond(
        early, lambda: begin(tok_len + width), lambda: begin(tok_len)
    )

    recv = lax.all_to_all(send, "context", 0, 0, axis_index_groups=[ORDER], tiled=True)

    constants = [jnp.asarray(table) for table in tables()]
    send = pl.pallas_call(
        convolve_kernel,
        out_shape=pltpu.VMEM((channels, PIECE, LANES), jnp.bfloat16),
        in_specs=whole(1 + len(constants)),
        out_specs=whole(1)[0],
        scratch_shapes=[
            pltpu.VMEM((ranks, 2 * PIECE, LANES), jnp.float32),
            pltpu.VMEM((channels, PIECE, LANES), jnp.float32),
        ],
        compiler_params=pltpu.CompilerParams(vmem_limit_bytes=24 * 2**20),
        name="convolve",
    )(recv, *constants)

    recv = lax.all_to_all(send, "context", 0, 0, axis_index_groups=HALVES, tiled=True)

    def finish(lanes):
        send = pl.pallas_call(
            gate_kernel,
            out_shape=pltpu.VMEM((groups, channels, lanes), jnp.bfloat16),
            in_specs=whole(4),
            out_specs=whole(1)[0],
            scratch_shapes=[pltpu.VMEM((channels, PIECE, LANES), jnp.float32)],
            compiler_params=pltpu.CompilerParams(vmem_limit_bytes=16 * 2**20),
            name="gate",
        )(*near(recv, gate, direct, proj_full))
        gathered = lax.all_to_all(send, "tensor", 0, 0, axis_index_groups=[GROUP], tiled=True)
        return pl.pallas_call(
            mix_kernel,
            out_shape=pltpu.HBM((width, tok_len), jnp.bfloat16),
            in_specs=whole(2),
            out_specs=whole(1)[0],
            compiler_params=pltpu.CompilerParams(vmem_limit_bytes=16 * 2**20),
            name="mix",
        )(*near(proj_full, gathered.reshape(width, lanes)))

    return lax.cond(early, lambda: finish(tok_len), lambda: finish(tok_len + width))


def solution(mesh):
    return jax.shard_map(
        shards,
        mesh=mesh,
        in_specs=(
            P("tensor", "context"),
            P(None, None, "tensor"),
            P("tensor", "context"),
            P("tensor"),
            P("tensor", None),
        ),
        out_specs=P(None, "context"),
        check_vma=False,
    )
```

```python
import math

import jax
import jax.numpy as jnp
import numpy as np
from jax import lax
from jax.experimental import pallas as pl
from jax.experimental.pallas import tpu as pltpu
from jax.sharding import PartitionSpec as P

ROWS = 256
LANES = 128
LENGTH = ROWS * LANES
PIECE = 4
RANKS = ROWS // PIECE
LINES, RING = 4, 16
CHANNELS = RANKS // 2

TURN = 2
HALVES = [
    [(outer + TURN) % LINES * RING + inner for outer in range(LINES) for inner in ring]
    for ring in ((10, 11, 12, 13, 14, 15, 8, 9), (6, 7, 5, 4, 3, 2, 1, 0))
]
ORDER = HALVES[0][:1] + HALVES[1] + HALVES[0][1:]

GROUP = [5, 4, 6, 7, 0, 1, 2, 3]


def split_table(table):
    upper = table.astype(jnp.bfloat16)
    lower = (table - upper.astype(np.float64)).astype(jnp.bfloat16)
    return upper, lower


def tables():
    come = np.concatenate([np.asarray(ORDER) * PIECE + piece for piece in range(PIECE)])
    go = np.concatenate(
        [np.asarray(half) * PIECE + piece for half in HALVES for piece in range(PIECE)]
    )
    low = np.arange(ROWS)
    lane = np.arange(LANES)

    def outer(row):
        turn = 2.0 * np.pi * np.outer(low + 0.25, row) / ROWS
        return np.concatenate([np.cos(turn), -np.sin(turn)], axis=0)

    turn = 2.0 * np.pi * np.outer(low + 0.25, lane) / LENGTH
    twist = np.stack([np.cos(turn), np.sin(turn)]).astype(np.float32)
    turn = 2.0 * np.pi * (np.outer(lane, lane) % LANES) / LANES
    cos_part, sin_part = np.cos(turn), np.sin(turn)
    inner = np.block([[cos_part, -sin_part], [sin_part, cos_part]])
    return (
        *split_table(outer(come)),
        *split_table(outer(go).T / LENGTH),
        *split_table(inner),
        *split_table(inner.T),
        twist,
    )


def dot(left, right):
    return jnp.dot(left, right, preferred_element_type=jnp.float32)


def split_value(value):
    upper = value.astype(jnp.bfloat16)
    lower = (value - upper.astype(jnp.float32)).astype(jnp.bfloat16)
    return upper, lower


def halves(part, rows):
    middle = rows // 2
    return jnp.concatenate([part(slice(0, middle)), part(slice(middle, rows))], axis=0)


def inner_transform(value, table_hi, table_lo):
    upper, lower = split_value(value)
    return halves(
        lambda cut: dot(upper[cut], table_hi[...])
        + dot(lower[cut], table_hi[...])
        + dot(upper[cut], table_lo[...]),
        value.shape[0],
    )


def spread_kernel(
    sequence_ref, proj_ref, filter_ref, skip_ref, out_ref,
    send_ref, proj_copy, filter_copy, skip_copy, out_copy,
):
    tok_len = sequence_ref.shape[1]
    for copy in range(send_ref.shape[0]):
        send_ref[copy, :, :tok_len] = sequence_ref[...]
        if send_ref.shape[2] > tok_len:
            send_ref[copy, :, tok_len:] = out_ref[...]
    proj_copy[...] = proj_ref[...]
    filter_copy[...] = filter_ref[...]
    skip_copy[...] = skip_ref[...]
    out_copy[...] = out_ref[...]


def project_kernel(
    gathered_ref, proj_ref, filter_ref, skip_ref, own_ref,
    send_ref, gate_ref, direct_ref, out_ref, rows_ref,
):
    channels, tok_len = filter_ref.shape
    sequence = jnp.concatenate(
        [
            gathered_ref[place * channels : (place + 1) * channels, :tok_len]
            for place in np.argsort(GROUP).tolist()
        ],
        axis=0,
    )
    first, gate, value = [dot(proj_ref[index], sequence) for index in range(3)]
    gated = value * first
    gate_ref[...] = gate
    place = lax.broadcasted_iota(jnp.int32, (channels, channels), 0)
    other = lax.broadcasted_iota(jnp.int32, (channels, channels), 1)
    skip = jnp.sum(jnp.where(place == other, skip_ref[...], 0.0), axis=1, keepdims=True)
    direct_ref[...] = skip * gated
    if gathered_ref.shape[1] > tok_len:
        out_ref[...] = gathered_ref[:, tok_len:]
    else:
        out_ref[:channels] = own_ref[...]
    for piece in range(PIECE):
        cut = slice(piece * LANES, (piece + 1) * LANES)
        rows_ref[:, piece, :] = gated[:, cut]
        rows_ref[:, PIECE + piece, :] = filter_ref[:, cut]
    rows = rows_ref[...].astype(jnp.bfloat16)
    send_ref[:1] = rows[:1]
    send_ref[1 : channels + 1] = rows
    send_ref[channels + 1 :] = rows[1:]


def convolve_kernel(
    recv_ref, fwd_hi, fwd_lo, back_hi, back_lo, in_hi, in_lo, out_hi, out_lo, twist_ref,
    send_ref, rows_ref, result_ref,
):
    rows_ref[...] = recv_ref[...].astype(jnp.float32)
    both = jnp.concatenate(
        [
            jnp.concatenate([rows_ref[:, piece, :], rows_ref[:, PIECE + piece, :]], axis=1)
            for piece in range(PIECE)
        ],
        axis=0,
    ).astype(jnp.bfloat16)
    cos_part = twist_ref[0]
    sin_part = twist_ref[1]
    outer = halves(lambda cut: dot(fwd_hi[cut], both) + dot(fwd_lo[cut], both), 2 * ROWS)
    real, imag = outer[:ROWS], outer[ROWS:]
    turned = []
    for cut in (slice(0, LANES), slice(LANES, 2 * LANES)):
        turned.append(
            jnp.concatenate(
                [
                    real[:, cut] * cos_part + imag[:, cut] * sin_part,
                    imag[:, cut] * cos_part - real[:, cut] * sin_part,
                ],
                axis=1,
            )
        )
    spectra = inner_transform(jnp.concatenate(turned, axis=0), in_hi, in_lo)
    source_real, source_imag = spectra[:ROWS, :LANES], spectra[:ROWS, LANES:]
    filter_real, filter_imag = spectra[ROWS:, :LANES], spectra[ROWS:, LANES:]
    product = jnp.concatenate(
        [
            source_real * filter_real - source_imag * filter_imag,
            source_real * filter_imag + source_imag * filter_real,
        ],
        axis=1,
    )
    inner = inner_transform(product, out_hi, out_lo)
    real, imag = inner[:, :LANES], inner[:, LANES:]
    upper, lower = split_value(
        jnp.concatenate(
            [real * cos_part - imag * sin_part, imag * cos_part + real * sin_part], axis=0
        )
    )
    half = 1 - lax.axis_index("context") % RING // (RING // 2)
    span = pl.ds(pl.multiple_of(half * (ROWS // 2), ROWS // 2), ROWS // 2)
    both = dot(back_hi[span, :], jnp.concatenate([upper, lower], axis=1))
    result = both[:, :LANES] + both[:, LANES:] + dot(back_lo[span, :], upper)
    for piece in range(PIECE):
        result_ref[:, piece, :] = result[piece * CHANNELS : (piece + 1) * CHANNELS]
    send_ref[...] = result_ref[...].astype(jnp.bfloat16)


def gate_kernel(recv_ref, gate_ref, direct_ref, out_ref, send_ref, rows_ref):
    channels, tok_len = gate_ref.shape
    rows_ref[...] = recv_ref[...].astype(jnp.float32)
    convolved = jnp.concatenate([rows_ref[:, piece, :] for piece in range(PIECE)], axis=1)
    out_gated = ((convolved + direct_ref[...]) * gate_ref[...]).astype(jnp.bfloat16)
    for copy in range(send_ref.shape[0]):
        send_ref[copy, :, :tok_len] = out_gated
        if send_ref.shape[2] > tok_len:
            send_ref[copy, :, tok_len:] = out_ref[:channels]


def mix_kernel(out_ref, gathered_ref, mixed_ref):
    tok_len = mixed_ref.shape[1]
    late = gathered_ref.shape[1] > tok_len
    mixed_ref[...] = lax.dot_general(
        gathered_ref[:, tok_len:] if late else out_ref[...],
        gathered_ref[:, :tok_len],
        (((0,), (0,)), ((), ())),
        preferred_element_type=jnp.float32,
    ).astype(jnp.bfloat16)


def near(*arrays):
    return [pltpu.with_memory_space_constraint(array, pltpu.VMEM) for array in arrays]


def far(*arrays):
    return [pltpu.with_memory_space_constraint(array, pltpu.HBM) for array in arrays]


def whole(count):
    return [pl.BlockSpec(memory_space=pltpu.VMEM) for _ in range(count)]


def shards(sequence, proj_in, conv_filter, skip_gain, proj_out):
    channels, tok_len = sequence.shape
    width = proj_out.shape[1]
    groups = lax.axis_size("tensor")
    ranks = lax.axis_size("context")

    early = lax.axis_index("context") % RING < RING // 2

    def begin(lanes):
        operands = [
            sequence,
            jnp.swapaxes(proj_in, 1, 2),
            conv_filter,
            skip_gain.reshape(1, channels),
            proj_out,
        ]
        send, *local = pl.pallas_call(
            spread_kernel,
            out_shape=(
                pltpu.VMEM((groups, channels, lanes), jnp.bfloat16),
                *[pltpu.VMEM(operand.shape, operand.dtype) for operand in operands[1:]],
            ),
            in_specs=whole(5),
            out_specs=tuple(whole(5)),
            name="spread",
        )(*far(*operands))
        gathered = lax.all_to_all(send, "tensor", 0, 0, axis_index_groups=[GROUP], tiled=True)
        return tuple(
            pl.pallas_call(
                project_kernel,
                out_shape=(
                    pltpu.VMEM((ranks, 2 * PIECE, LANES), jnp.bfloat16),
                    pltpu.VMEM((channels, tok_len), jnp.float32),
                    pltpu.VMEM((channels, tok_len), jnp.float32),
                    pltpu.VMEM((width, width), jnp.bfloat16),
                ),
                in_specs=whole(5),
                out_specs=tuple(whole(4)),
                scratch_shapes=[pltpu.VMEM((channels, 2 * PIECE, LANES), jnp.float32)],
                compiler_params=pltpu.CompilerParams(vmem_limit_bytes=16 * 2**20),
                name="project",
            )(*near(gathered.reshape(width, lanes), *local))
        )

    send, gate, direct, proj_full = lax.cond(
        early, lambda: begin(tok_len + width), lambda: begin(tok_len)
    )

    recv = lax.all_to_all(send, "context", 0, 0, axis_index_groups=[ORDER], tiled=True)

    constants = [jnp.asarray(table) for table in tables()]
    send = pl.pallas_call(
        convolve_kernel,
        out_shape=pltpu.VMEM((channels, PIECE, LANES), jnp.bfloat16),
        in_specs=whole(1 + len(constants)),
        out_specs=whole(1)[0],
        scratch_shapes=[
            pltpu.VMEM((ranks, 2 * PIECE, LANES), jnp.float32),
            pltpu.VMEM((channels, PIECE, LANES), jnp.float32),
        ],
        compiler_params=pltpu.CompilerParams(vmem_limit_bytes=24 * 2**20),
        name="convolve",
    )(recv, *constants)

    recv = lax.all_to_all(send, "context", 0, 0, axis_index_groups=HALVES, tiled=True)

    def finish(lanes):
        send = pl.pallas_call(
            gate_kernel,
            out_shape=pltpu.VMEM((groups, channels, lanes), jnp.bfloat16),
            in_specs=whole(4),
            out_specs=whole(1)[0],
            scratch_shapes=[pltpu.VMEM((channels, PIECE, LANES), jnp.float32)],
            compiler_params=pltpu.CompilerParams(vmem_limit_bytes=16 * 2**20),
            name="gate",
        )(*near(recv, gate, direct, proj_full))
        gathered = lax.all_to_all(send, "tensor", 0, 0, axis_index_groups=[GROUP], tiled=True)
        return pl.pallas_call(
            mix_kernel,
            out_shape=pltpu.HBM((width, tok_len), jnp.bfloat16),
            in_specs=whole(2),
            out_specs=whole(1)[0],
            compiler_params=pltpu.CompilerParams(vmem_limit_bytes=16 * 2**20),
            name="mix",
        )(*near(proj_full, gathered.reshape(width, lanes)))

    return lax.cond(early, lambda: finish(tok_len), lambda: finish(tok_len + width))


def solution(mesh):
    return jax.shard_map(
        shards,
        mesh=mesh,
        in_specs=(
            P("tensor", "context"),
            P(None, None, "tensor"),
            P("tensor", "context"),
            P("tensor"),
            P("tensor", None),
        ),
        out_specs=P(None, "context"),
        check_vma=False,
    )
```

```python
import math

import jax
import jax.numpy as jnp
import numpy as np
from jax import lax
from jax.experimental import pallas as pl
from jax.experimental.pallas import tpu as pltpu
from jax.sharding import PartitionSpec as P

ROWS = 256
LANES = 128
LENGTH = ROWS * LANES
PIECE = 4
RANKS = ROWS // PIECE
LINES, RING = 4, 16
CHANNELS = RANKS // 2

TURN = 2
HALVES = [
    [(outer + TURN) % LINES * RING + inner for outer in range(LINES) for inner in ring]
    for ring in ((11, 12, 13, 14, 15, 8, 9, 10), (6, 7, 5, 4, 3, 2, 1, 0))
]
ORDER = HALVES[0] + HALVES[1]

EARLY = 3

GROUP = [5, 4, 6, 7, 0, 1, 2, 3]


def split_table(table):
    upper = table.astype(jnp.bfloat16)
    lower = (table - upper.astype(np.float64)).astype(jnp.bfloat16)
    return upper, lower


def tables():
    come = np.concatenate([np.asarray(ORDER) * PIECE + piece for piece in range(PIECE)])
    go = np.concatenate(
        [np.asarray(half) * PIECE + piece for half in HALVES for piece in range(PIECE)]
    )
    low = np.arange(ROWS)
    lane = np.arange(LANES)

    def outer(row):
        turn = 2.0 * np.pi * np.outer(low + 0.25, row) / ROWS
        return np.concatenate([np.cos(turn), -np.sin(turn)], axis=0)

    turn = 2.0 * np.pi * np.outer(low + 0.25, lane) / LENGTH
    twist = np.stack([np.cos(turn), np.sin(turn)]).astype(np.float32)
    turn = 2.0 * np.pi * (np.outer(lane, lane) % LANES) / LANES
    cos_part, sin_part = np.cos(turn), np.sin(turn)
    inner = np.block([[cos_part, -sin_part], [sin_part, cos_part]])
    return (
        *split_table(outer(come)),
        *split_table(outer(go).T / LENGTH),
        *split_table(inner),
        *split_table(inner.T),
        twist,
    )


def dot(left, right):
    return jnp.dot(left, right, preferred_element_type=jnp.float32)


def split_value(value):
    upper = value.astype(jnp.bfloat16)
    lower = (value - upper.astype(jnp.float32)).astype(jnp.bfloat16)
    return upper, lower


def halves(part, rows):
    middle = rows // 2
    return jnp.concatenate([part(slice(0, middle)), part(slice(middle, rows))], axis=0)


def inner_transform(value, table_hi, table_lo):
    upper, lower = split_value(value)
    return halves(
        lambda cut: dot(upper[cut], table_hi[...])
        + dot(lower[cut], table_hi[...])
        + dot(upper[cut], table_lo[...]),
        value.shape[0],
    )


def spread_kernel(
    sequence_ref, proj_ref, filter_ref, skip_ref, out_ref,
    send_ref, proj_copy, filter_copy, skip_copy, out_copy,
):
    tok_len = sequence_ref.shape[1]
    for copy in range(send_ref.shape[0]):
        send_ref[copy, :, :tok_len] = sequence_ref[...]
        if send_ref.shape[2] > tok_len:
            send_ref[copy, :, tok_len:] = out_ref[...]
    proj_copy[...] = proj_ref[...]
    filter_copy[...] = filter_ref[...]
    skip_copy[...] = skip_ref[...]
    out_copy[...] = out_ref[...]


def project_kernel(
    gathered_ref, proj_ref, filter_ref, skip_ref, own_ref,
    send_ref, gate_ref, direct_ref, out_ref, rows_ref,
):
    channels, tok_len = filter_ref.shape
    sequence = jnp.concatenate(
        [
            gathered_ref[place * channels : (place + 1) * channels, :tok_len]
            for place in np.argsort(GROUP).tolist()
        ],
        axis=0,
    )
    first, gate, value = [dot(proj_ref[index], sequence) for index in range(3)]
    gated = value * first
    gate_ref[...] = gate
    place = lax.broadcasted_iota(jnp.int32, (channels, channels), 0)
    other = lax.broadcasted_iota(jnp.int32, (channels, channels), 1)
    skip = jnp.sum(jnp.where(place == other, skip_ref[...], 0.0), axis=1, keepdims=True)
    direct_ref[...] = skip * gated
    if gathered_ref.shape[1] > tok_len:
        out_ref[...] = gathered_ref[:, tok_len:]
    else:
        out_ref[:channels] = own_ref[...]
    for piece in range(PIECE):
        cut = slice(piece * LANES, (piece + 1) * LANES)
        rows_ref[:, piece, :] = gated[:, cut]
        rows_ref[:, PIECE + piece, :] = filter_ref[:, cut]
    rows = rows_ref[...].astype(jnp.bfloat16)
    for half in range(2):
        send_ref[half * channels : (half + 1) * channels] = rows


def convolve_kernel(
    recv_ref, fwd_hi, fwd_lo, back_hi, back_lo, in_hi, in_lo, out_hi, out_lo, twist_ref,
    send_ref, rows_ref, result_ref,
):
    rows_ref[...] = recv_ref[...].astype(jnp.float32)
    both = jnp.concatenate(
        [
            jnp.concatenate([rows_ref[:, piece, :], rows_ref[:, PIECE + piece, :]], axis=1)
            for piece in range(PIECE)
        ],
        axis=0,
    ).astype(jnp.bfloat16)
    cos_part = twist_ref[0]
    sin_part = twist_ref[1]
    outer = halves(lambda cut: dot(fwd_hi[cut], both) + dot(fwd_lo[cut], both), 2 * ROWS)
    real, imag = outer[:ROWS], outer[ROWS:]
    turned = []
    for cut in (slice(0, LANES), slice(LANES, 2 * LANES)):
        turned.append(
            jnp.concatenate(
                [
                    real[:, cut] * cos_part + imag[:, cut] * sin_part,
                    imag[:, cut] * cos_part - real[:, cut] * sin_part,
                ],
                axis=1,
            )
        )
    spectra = inner_transform(jnp.concatenate(turned, axis=0), in_hi, in_lo)
    source_real, source_imag = spectra[:ROWS, :LANES], spectra[:ROWS, LANES:]
    filter_real, filter_imag = spectra[ROWS:, :LANES], spectra[ROWS:, LANES:]
    product = jnp.concatenate(
        [
            source_real * filter_real - source_imag * filter_imag,
            source_real * filter_imag + source_imag * filter_real,
        ],
        axis=1,
    )
    inner = inner_transform(product, out_hi, out_lo)
    real, imag = inner[:, :LANES], inner[:, LANES:]
    upper, lower = split_value(
        jnp.concatenate(
            [real * cos_part - imag * sin_part, imag * cos_part + real * sin_part], axis=0
        )
    )
    half = 1 - lax.axis_index("context") % RING // (RING // 2)
    span = pl.ds(pl.multiple_of(half * (ROWS // 2), ROWS // 2), ROWS // 2)
    both = dot(back_hi[span, :], jnp.concatenate([upper, lower], axis=1))
    result = both[:, :LANES] + both[:, LANES:] + dot(back_lo[span, :], upper)
    for piece in range(PIECE):
        result_ref[:, piece, :] = result[piece * CHANNELS : (piece + 1) * CHANNELS]
    send_ref[...] = result_ref[...].astype(jnp.bfloat16)


def gate_kernel(recv_ref, gate_ref, direct_ref, out_ref, send_ref, rows_ref):
    channels, tok_len = gate_ref.shape
    rows_ref[...] = recv_ref[...].astype(jnp.float32)
    convolved = jnp.concatenate([rows_ref[:, piece, :] for piece in range(PIECE)], axis=1)
    out_gated = ((convolved + direct_ref[...]) * gate_ref[...]).astype(jnp.bfloat16)
    for copy in range(send_ref.shape[0]):
        send_ref[copy, :, :tok_len] = out_gated
        if send_ref.shape[2] > tok_len:
            send_ref[copy, :, tok_len:] = out_ref[:channels]


def mix_kernel(out_ref, gathered_ref, mixed_ref):
    tok_len = mixed_ref.shape[1]
    late = gathered_ref.shape[1] > tok_len
    mixed_ref[...] = lax.dot_general(
        gathered_ref[:, tok_len:] if late else out_ref[...],
        gathered_ref[:, :tok_len],
        (((0,), (0,)), ((), ())),
        preferred_element_type=jnp.float32,
    ).astype(jnp.bfloat16)


def near(*arrays):
    return [pltpu.with_memory_space_constraint(array, pltpu.VMEM) for array in arrays]


def far(*arrays):
    return [pltpu.with_memory_space_constraint(array, pltpu.HBM) for array in arrays]


def whole(count):
    return [pl.BlockSpec(memory_space=pltpu.VMEM) for _ in range(count)]


def shards(sequence, proj_in, conv_filter, skip_gain, proj_out):
    channels, tok_len = sequence.shape
    width = proj_out.shape[1]
    groups = lax.axis_size("tensor")
    ranks = lax.axis_size("context")

    early = lax.axis_index("context") % RING < EARLY

    def begin(lanes):
        operands = [
            sequence,
            jnp.swapaxes(proj_in, 1, 2),
            conv_filter,
            skip_gain.reshape(1, channels),
            proj_out,
        ]
        send, *local = pl.pallas_call(
            spread_kernel,
            out_shape=(
                pltpu.VMEM((groups, channels, lanes), jnp.bfloat16),
                *[pltpu.VMEM(operand.shape, operand.dtype) for operand in operands[1:]],
            ),
            in_specs=whole(5),
            out_specs=tuple(whole(5)),
            name="spread",
        )(*far(*operands))
        gathered = lax.all_to_all(send, "tensor", 0, 0, axis_index_groups=[GROUP], tiled=True)
        return tuple(
            pl.pallas_call(
                project_kernel,
                out_shape=(
                    pltpu.VMEM((ranks, 2 * PIECE, LANES), jnp.bfloat16),
                    pltpu.VMEM((channels, tok_len), jnp.float32),
                    pltpu.VMEM((channels, tok_len), jnp.float32),
                    pltpu.VMEM((width, width), jnp.bfloat16),
                ),
                in_specs=whole(5),
                out_specs=tuple(whole(4)),
                scratch_shapes=[pltpu.VMEM((channels, 2 * PIECE, LANES), jnp.float32)],
                compiler_params=pltpu.CompilerParams(vmem_limit_bytes=16 * 2**20),
                name="project",
            )(*near(gathered.reshape(width, lanes), *local))
        )

    send, gate, direct, proj_full = lax.cond(
        early, lambda: begin(tok_len + width), lambda: begin(tok_len)
    )

    recv = lax.all_to_all(send, "context", 0, 0, axis_index_groups=[ORDER], tiled=True)

    constants = [jnp.asarray(table) for table in tables()]
    send = pl.pallas_call(
        convolve_kernel,
        out_shape=pltpu.VMEM((channels, PIECE, LANES), jnp.bfloat16),
        in_specs=whole(1 + len(constants)),
        out_specs=whole(1)[0],
        scratch_shapes=[
            pltpu.VMEM((ranks, 2 * PIECE, LANES), jnp.float32),
            pltpu.VMEM((channels, PIECE, LANES), jnp.float32),
        ],
        compiler_params=pltpu.CompilerParams(vmem_limit_bytes=24 * 2**20),
        name="convolve",
    )(recv, *constants)

    recv = lax.all_to_all(send, "context", 0, 0, axis_index_groups=HALVES, tiled=True)

    def finish(lanes):
        send = pl.pallas_call(
            gate_kernel,
            out_shape=pltpu.VMEM((groups, channels, lanes), jnp.bfloat16),
            in_specs=whole(4),
            out_specs=whole(1)[0],
            scratch_shapes=[pltpu.VMEM((channels, PIECE, LANES), jnp.float32)],
            compiler_params=pltpu.CompilerParams(vmem_limit_bytes=16 * 2**20),
            name="gate",
        )(*near(recv, gate, direct, proj_full))
        gathered = lax.all_to_all(send, "tensor", 0, 0, axis_index_groups=[GROUP], tiled=True)
        return pl.pallas_call(
            mix_kernel,
            out_shape=pltpu.HBM((width, tok_len), jnp.bfloat16),
            in_specs=whole(2),
            out_specs=whole(1)[0],
            compiler_params=pltpu.CompilerParams(vmem_limit_bytes=16 * 2**20),
            name="mix",
        )(*near(proj_full, gathered.reshape(width, lanes)))

    return lax.cond(early, lambda: finish(tok_len), lambda: finish(tok_len + width))


def solution(mesh):
    return jax.shard_map(
        shards,
        mesh=mesh,
        in_specs=(
            P("tensor", "context"),
            P(None, None, "tensor"),
            P("tensor", "context"),
            P("tensor"),
            P("tensor", None),
        ),
        out_specs=P(None, "context"),
        check_vma=False,
    )
```

```python
import math

import jax
import jax.numpy as jnp
import numpy as np
from jax import lax
from jax.experimental import pallas as pl
from jax.experimental.pallas import tpu as pltpu
from jax.sharding import PartitionSpec as P

ROWS = 256
LANES = 128
LENGTH = ROWS * LANES
PIECE = 4
RANKS = ROWS // PIECE
LINES, RING = 4, 16
CHANNELS = RANKS // 2

TURN = 2
HALVES = [
    [(outer + TURN) % LINES * RING + inner for outer in range(LINES) for inner in ring]
    for ring in ((10, 11, 12, 13, 14, 15, 8, 9), (6, 5, 4, 7, 3, 2, 1, 0))
]
ORDER = HALVES[0] + HALVES[1]

GROUP = [5, 4, 6, 7, 0, 1, 2, 3]


def split_table(table):
    upper = table.astype(jnp.bfloat16)
    lower = (table - upper.astype(np.float64)).astype(jnp.bfloat16)
    return upper, lower


def tables():
    come = np.concatenate([np.asarray(ORDER) * PIECE + piece for piece in range(PIECE)])
    go = np.concatenate(
        [np.asarray(half) * PIECE + piece for half in HALVES for piece in range(PIECE)]
    )
    low = np.arange(ROWS)
    lane = np.arange(LANES)

    def outer(row):
        turn = 2.0 * np.pi * np.outer(low + 0.25, row) / ROWS
        return np.concatenate([np.cos(turn), -np.sin(turn)], axis=0)

    turn = 2.0 * np.pi * np.outer(low + 0.25, lane) / LENGTH
    twist = np.stack([np.cos(turn), np.sin(turn)]).astype(np.float32)
    turn = 2.0 * np.pi * (np.outer(lane, lane) % LANES) / LANES
    cos_part, sin_part = np.cos(turn), np.sin(turn)
    inner = np.block([[cos_part, -sin_part], [sin_part, cos_part]])
    return (
        *split_table(outer(come)),
        *split_table(outer(go).T / LENGTH),
        *split_table(inner),
        *split_table(inner.T),
        twist,
    )


def dot(left, right):
    return jnp.dot(left, right, preferred_element_type=jnp.float32)


def split_value(value):
    upper = value.astype(jnp.bfloat16)
    lower = (value - upper.astype(jnp.float32)).astype(jnp.bfloat16)
    return upper, lower


def halves(part, rows):
    middle = rows // 2
    return jnp.concatenate([part(slice(0, middle)), part(slice(middle, rows))], axis=0)


def inner_transform(value, table_hi, table_lo):
    upper, lower = split_value(value)
    return halves(
        lambda cut: dot(upper[cut], table_hi[...])
        + dot(lower[cut], table_hi[...])
        + dot(upper[cut], table_lo[...]),
        value.shape[0],
    )


def spread_kernel(
    sequence_ref, proj_ref, filter_ref, skip_ref, out_ref,
    send_ref, proj_copy, filter_copy, skip_copy, out_copy,
):
    tok_len = sequence_ref.shape[1]
    for copy in range(send_ref.shape[0]):
        send_ref[copy, :, :tok_len] = sequence_ref[...]
        if send_ref.shape[2] > tok_len:
            send_ref[copy, :, tok_len:] = out_ref[...]
    proj_copy[...] = proj_ref[...]
    filter_copy[...] = filter_ref[...]
    skip_copy[...] = skip_ref[...]
    out_copy[...] = out_ref[...]


def project_kernel(
    gathered_ref, proj_ref, filter_ref, skip_ref, own_ref,
    send_ref, gate_ref, direct_ref, out_ref, rows_ref,
):
    channels, tok_len = filter_ref.shape
    sequence = jnp.concatenate(
        [
            gathered_ref[place * channels : (place + 1) * channels, :tok_len]
            for place in np.argsort(GROUP).tolist()
        ],
        axis=0,
    )
    first, gate, value = [dot(proj_ref[index], sequence) for index in range(3)]
    gated = value * first
    gate_ref[...] = gate
    place = lax.broadcasted_iota(jnp.int32, (channels, channels), 0)
    other = lax.broadcasted_iota(jnp.int32, (channels, channels), 1)
    skip = jnp.sum(jnp.where(place == other, skip_ref[...], 0.0), axis=1, keepdims=True)
    direct_ref[...] = skip * gated
    if gathered_ref.shape[1] > tok_len:
        out_ref[...] = gathered_ref[:, tok_len:]
    else:
        out_ref[:channels] = own_ref[...]
        out_ref[channels:] = jnp.zeros_like(out_ref[channels:])
    for piece in range(PIECE):
        cut = slice(piece * LANES, (piece + 1) * LANES)
        for half in range(2):
            span = slice(half * channels, (half + 1) * channels)
            rows_ref[span, piece, :] = gated[:, cut]
            rows_ref[span, PIECE + piece, :] = filter_ref[:, cut]
    send_ref[...] = rows_ref[...].astype(jnp.bfloat16)


def convolve_kernel(
    recv_ref, fwd_hi, fwd_lo, back_hi, back_lo, in_hi, in_lo, out_hi, out_lo, twist_ref,
    send_ref, rows_ref, result_ref,
):
    rows_ref[...] = recv_ref[...].astype(jnp.float32)
    both = jnp.concatenate(
        [
            jnp.concatenate([rows_ref[:, piece, :], rows_ref[:, PIECE + piece, :]], axis=1)
            for piece in range(PIECE)
        ],
        axis=0,
    ).astype(jnp.bfloat16)
    cos_part = twist_ref[0]
    sin_part = twist_ref[1]
    outer = halves(lambda cut: dot(fwd_hi[cut], both) + dot(fwd_lo[cut], both), 2 * ROWS)
    real, imag = outer[:ROWS], outer[ROWS:]
    turned = []
    for cut in (slice(0, LANES), slice(LANES, 2 * LANES)):
        turned.append(
            jnp.concatenate(
                [
                    real[:, cut] * cos_part + imag[:, cut] * sin_part,
                    imag[:, cut] * cos_part - real[:, cut] * sin_part,
                ],
                axis=1,
            )
        )
    spectra = inner_transform(jnp.concatenate(turned, axis=0), in_hi, in_lo)
    source_real, source_imag = spectra[:ROWS, :LANES], spectra[:ROWS, LANES:]
    filter_real, filter_imag = spectra[ROWS:, :LANES], spectra[ROWS:, LANES:]
    product = jnp.concatenate(
        [
            source_real * filter_real - source_imag * filter_imag,
            source_real * filter_imag + source_imag * filter_real,
        ],
        axis=1,
    )
    inner = inner_transform(product, out_hi, out_lo)
    real, imag = inner[:, :LANES], inner[:, LANES:]
    upper, lower = split_value(
        jnp.concatenate(
            [real * cos_part - imag * sin_part, imag * cos_part + real * sin_part], axis=0
        )
    )
    half = 1 - lax.axis_index("context") % RING // (RING // 2)
    span = pl.ds(pl.multiple_of(half * (ROWS // 2), ROWS // 2), ROWS // 2)
    both = dot(back_hi[span, :], jnp.concatenate([upper, lower], axis=1))
    result = both[:, :LANES] + both[:, LANES:] + dot(back_lo[span, :], upper)
    for piece in range(PIECE):
        result_ref[:, piece, :] = result[piece * CHANNELS : (piece + 1) * CHANNELS]
    send_ref[...] = result_ref[...].astype(jnp.bfloat16)


def gate_kernel(recv_ref, gate_ref, direct_ref, out_ref, send_ref, rows_ref):
    channels, tok_len = gate_ref.shape
    rows_ref[...] = recv_ref[...].astype(jnp.float32)
    convolved = jnp.concatenate([rows_ref[:, piece, :] for piece in range(PIECE)], axis=1)
    out_gated = ((convolved + direct_ref[...]) * gate_ref[...]).astype(jnp.bfloat16)
    for copy in range(send_ref.shape[0]):
        send_ref[copy, :, :tok_len] = out_gated
        if send_ref.shape[2] > tok_len:
            send_ref[copy, :, tok_len:] = out_ref[:channels]


def mix_kernel(out_ref, gathered_ref, mixed_ref):
    tok_len = mixed_ref.shape[1]
    late = gathered_ref.shape[1] > tok_len
    mixed_ref[...] = lax.dot_general(
        gathered_ref[:, tok_len:] if late else out_ref[...],
        gathered_ref[:, :tok_len],
        (((0,), (0,)), ((), ())),
        preferred_element_type=jnp.float32,
    ).astype(jnp.bfloat16)


def near(*arrays):
    return [pltpu.with_memory_space_constraint(array, pltpu.VMEM) for array in arrays]


def far(*arrays):
    return [pltpu.with_memory_space_constraint(array, pltpu.HBM) for array in arrays]


def whole(count):
    return [pl.BlockSpec(memory_space=pltpu.VMEM) for _ in range(count)]


def shards(sequence, proj_in, conv_filter, skip_gain, proj_out):
    channels, tok_len = sequence.shape
    width = proj_out.shape[1]
    groups = lax.axis_size("tensor")
    ranks = lax.axis_size("context")

    early = lax.axis_index("context") % RING < RING // 2

    def begin(lanes):
        operands = [
            sequence,
            jnp.swapaxes(proj_in, 1, 2),
            conv_filter,
            skip_gain.reshape(1, channels),
            proj_out,
        ]
        send, *local = pl.pallas_call(
            spread_kernel,
            out_shape=(
                pltpu.VMEM((groups, channels, lanes), jnp.bfloat16),
                *[pltpu.VMEM(operand.shape, operand.dtype) for operand in operands[1:]],
            ),
            in_specs=whole(5),
            out_specs=tuple(whole(5)),
            name="spread",
        )(*far(*operands))
        gathered = lax.all_to_all(send, "tensor", 0, 0, axis_index_groups=[GROUP], tiled=True)
        return tuple(
            pl.pallas_call(
                project_kernel,
                out_shape=(
                    pltpu.VMEM((ranks, 2 * PIECE, LANES), jnp.bfloat16),
                    pltpu.VMEM((channels, tok_len), jnp.float32),
                    pltpu.VMEM((channels, tok_len), jnp.float32),
                    pltpu.VMEM((width, width), jnp.bfloat16),
                ),
                in_specs=whole(5),
                out_specs=tuple(whole(4)),
                scratch_shapes=[pltpu.VMEM((ranks, 2 * PIECE, LANES), jnp.float32)],
                compiler_params=pltpu.CompilerParams(vmem_limit_bytes=16 * 2**20),
                name="project",
            )(*near(gathered.reshape(width, lanes), *local))
        )

    send, gate, direct, proj_full = lax.cond(
        early, lambda: begin(tok_len + width), lambda: begin(tok_len)
    )

    recv = lax.all_to_all(send, "context", 0, 0, axis_index_groups=[ORDER], tiled=True)

    constants = [jnp.asarray(table) for table in tables()]
    send = pl.pallas_call(
        convolve_kernel,
        out_shape=pltpu.VMEM((channels, PIECE, LANES), jnp.bfloat16),
        in_specs=whole(1 + len(constants)),
        out_specs=whole(1)[0],
        scratch_shapes=[
            pltpu.VMEM((ranks, 2 * PIECE, LANES), jnp.float32),
            pltpu.VMEM((channels, PIECE, LANES), jnp.float32),
        ],
        compiler_params=pltpu.CompilerParams(vmem_limit_bytes=24 * 2**20),
        name="convolve",
    )(recv, *constants)

    recv = lax.all_to_all(send, "context", 0, 0, axis_index_groups=HALVES, tiled=True)

    def finish(lanes):
        send = pl.pallas_call(
            gate_kernel,
            out_shape=pltpu.VMEM((groups, channels, lanes), jnp.bfloat16),
            in_specs=whole(4),
            out_specs=whole(1)[0],
            scratch_shapes=[pltpu.VMEM((channels, PIECE, LANES), jnp.float32)],
            compiler_params=pltpu.CompilerParams(vmem_limit_bytes=16 * 2**20),
            name="gate",
        )(*near(recv, gate, direct, proj_full))
        gathered = lax.all_to_all(send, "tensor", 0, 0, axis_index_groups=[GROUP], tiled=True)
        return pl.pallas_call(
            mix_kernel,
            out_shape=pltpu.HBM((width, tok_len), jnp.bfloat16),
            in_specs=whole(2),
            out_specs=whole(1)[0],
            compiler_params=pltpu.CompilerParams(vmem_limit_bytes=16 * 2**20),
            name="mix",
        )(*near(proj_full, gathered.reshape(width, lanes)))

    return lax.cond(early, lambda: finish(tok_len), lambda: finish(tok_len + width))


def solution(mesh):
    return jax.shard_map(
        shards,
        mesh=mesh,
        in_specs=(
            P("tensor", "context"),
            P(None, None, "tensor"),
            P("tensor", "context"),
            P("tensor"),
            P("tensor", None),
        ),
        out_specs=P(None, "context"),
        check_vma=False,
    )
```
